32 devices in a mesh: groups: 2 (over y), ex: 4 (over z), feat: 2 (over x), pb: 2 (over core).
Axes of the slice: x: 2, y: 2, z: 4, core: 2. Of those that a mesh axis runs over, the one named last changes fastest.
Arguments:
- activations: bfloat16 [8, 4, 128, 4096], P(('groups', 'ex'), ('feat', 'pb')), parts along dimension 0, may hold values from -6 to 6
- out_grads: bfloat16 [8, 4, 128, 7168], P(('groups', 'ex'), ('feat', 'pb')), parts along dimension 0
- act_proj: bfloat16 [4096, 64], replicated
- grad_proj: bfloat16 [7168, 64], replicated
- tok_counts: int32 [8, 4], P(('groups', 'ex'), ('feat', 'pb')), parts along dimension 0, may hold values from 1 to 128, as said below
- example_ids: int32 [8, 4], P('groups', ('feat', 'pb')), parts along dimension 0, may hold values from 0 to 15, as said below
- query_sketch: bfloat16 [2048, 4096], P(('groups', 'pb'), 'ex'), parts along dimension 0, may hold values from -6 to 6
- query_ids: int32 [2048], P('groups'), parts along dimension 0, may hold values from 0 to 31
Outputs:
- gram: float32 [8192, 4096], P(('groups', 'ex'), ('feat', 'pb')), parts along dimension 0
- scores: float32 [2048, 4, 4], P(('groups', 'ex'), None, ('feat', 'pb')), parts along dimension 0
The draws below stay inside these ranges and needn't reach their ends.
There are 2 independent parts, one for each index of `groups`. The reference program is written for one: setup_inputs(seed, part) draws one part's arguments, and reference() takes and returns one part's arrays. A program takes and returns all parts, laid end to end along the dimension named above; an argument that names none is the same for every part. Nothing has to cross between parts.
Inputs may be any that keep to these rules, and one draw needn't show every extreme that they name: `tok_counts`: some example has all 128 tokens live. `example_ids`: all different.
All inputs are finite; a program needn't handle non-finite values.
Results may differ from the reference program's by a relative error of at most 0.0075.
Values may be sent and summed in bfloat16 or wider, within the bound.
No kernel may reach another device: no remote copies, remote signals or barrier semaphores. Data moves between devices by JAX's collectives and lax.ppermute only.
A program may use at most 64 MiB of HBM per device.

```python
import math
import jax
import jax.numpy as jnp
from jax import lax

D = 4096
FW = 7168
R = 64
SEQ = 128
NQ = 1024
K = 4096
EXA = 4
EXB = 4
EXAMPLES = 16


def draw_act_proj(key, part):
    key = jax.random.fold_in(key, 5)
    first_key, second_key = jax.random.split(key)
    base = jax.random.normal(first_key, (D, R), jnp.float32)
    spread = jnp.exp(jax.random.uniform(second_key, (R,), jnp.float32, -0.6931472, 0.6931472))
    return (base * spread[None, :] / math.sqrt(D)).astype(jnp.bfloat16)


def draw_grad_proj(key, part):
    key = jax.random.fold_in(key, 6)
    first_key, second_key = jax.random.split(key)
    base = jax.random.normal(first_key, (FW, R), jnp.float32)
    spread = jnp.exp(jax.random.uniform(second_key, (R,), jnp.float32, -0.6931472, 0.6931472))
    return (base * spread[None, :] / math.sqrt(FW)).astype(jnp.bfloat16)


def draw_out_grads(key, part):
    key = jax.random.fold_in(key, 7)
    first_key = jax.random.fold_in(key, 0)
    rising = 0.6 * 3.0 ** (jnp.arange(EXA, dtype=jnp.float32) / max(EXA - 1, 1))
    base = jax.random.normal(first_key, (EXA, EXB, SEQ, FW), jnp.float32)
    return (base * rising[:, None, None, None]).astype(jnp.bfloat16)


def draw_tok_counts(key, part):
    key = jax.random.fold_in(key, 11)
    counts_drawn = jax.random.randint(key, (EXA, EXB), 1, SEQ + 1, jnp.int32)
    return counts_drawn.at[0, 0].set(SEQ)


def draw_example_ids(key, part):
    key = jax.random.fold_in(key, 13)
    return jax.random.permutation(key, EXAMPLES).astype(jnp.int32).reshape(EXA, EXB)


def plant(result, own_key, low, high):
    dims = result.shape
    spot = [jax.random.randint(jax.random.fold_in(own_key, axis), (), 0, dims[axis]) for axis in range(len(dims))]
    result = result.at[tuple(spot)].set(low)
    longest = dims.index(max(dims))
    spot[longest] = (spot[longest] + 1) % dims[longest]
    return result.at[tuple(spot)].set(high)


def block_scale(key, extent, cuts, low, top_value):
    loudness, own = 1.0, jax.random.fold_in(key, 6)
    for dim, blocks in cuts:
        heights = jnp.exp(jax.random.uniform(jax.random.fold_in(own, dim), (blocks,), jnp.float32, low / len(cuts), top_value / len(cuts)))
        loudness = loudness * jnp.repeat(heights, extent[dim] // blocks).reshape([-1 if axis == dim else 1 for axis in range(len(extent))])
    return loudness


def normal_values(rng, dims, width, limit, shards=(), kind=jnp.bfloat16):
    values = jax.random.normal(rng, dims, jnp.float32) * width
    if len(shards) > 0:
        values = block_scale(rng, dims, shards, -0.22, 0.18) * values
    return jnp.clip(values, min=-limit, max=limit).astype(kind)


def setup_inputs(seed: int = 0, part: int = 0) -> dict:
    keys = jax.random.split(jax.random.key(seed), 9)
    part_keys = jax.random.split(jax.random.fold_in(keys[8], part), 9)
    return {
        "activations": normal_values(part_keys[0], (EXA, EXB, SEQ, D), 1.0, 6.0, ((0, 4), (1, 4))),
        "out_grads": draw_out_grads(jax.random.fold_in(jax.random.fold_in(keys[8], part), 71), part),
        "act_proj": draw_act_proj(jax.random.fold_in(keys[8], 71), part),
        "grad_proj": draw_grad_proj(jax.random.fold_in(keys[8], 71), part),
        "tok_counts": draw_tok_counts(jax.random.fold_in(jax.random.fold_in(keys[8], part), 71), part),
        "example_ids": draw_example_ids(jax.random.fold_in(jax.random.fold_in(keys[8], part), 71), part),
        "query_sketch": normal_values(part_keys[6], (NQ, K), 1.0, 6.0, ((0, 2), (1, 4))),
        "query_ids": plant(jax.random.randint(part_keys[7], (NQ,), 0, 2 * EXAMPLES), jax.random.fold_in(part_keys[7], 1), 0, (2 * EXAMPLES) - 1).astype(jnp.int32),
    }


DAMPING = 0.1

def reference(activations, out_grads, act_proj, grad_proj, tok_counts, example_ids, query_sketch, query_ids):
    inputs_flat = activations.reshape(EXAMPLES, SEQ, D)
    grads_flat = out_grads.reshape(EXAMPLES, SEQ, FW)
    counts_flat = tok_counts.reshape(EXAMPLES)

    def sketch_one(items):
        tokens_in, grads_in, live_count = items
        act_low = jnp.dot(tokens_in, act_proj, preferred_element_type=jnp.float32).astype(jnp.bfloat16)
        grad_low = jnp.dot(grads_in, grad_proj, preferred_element_type=jnp.float32).astype(jnp.bfloat16)
        keep_mask = (jnp.arange(SEQ, dtype=jnp.int32) < live_count).astype(jnp.bfloat16)
        kept = grad_low * keep_mask[:, None]
        outer_sum = jnp.dot(kept.T, act_low, preferred_element_type=jnp.float32) * (1.0 / math.sqrt(SEQ))
        return outer_sum.reshape(R * R).astype(jnp.bfloat16)
    sketch = lax.map(sketch_one, (inputs_flat, grads_flat, counts_flat))
    gram = jnp.dot(sketch.T, sketch, preferred_element_type=jnp.float32) / EXAMPLES
    sketch_float = sketch.astype(jnp.float32)
    diag = lax.optimization_barrier(jnp.sum(sketch_float * sketch_float, axis=0)) / EXAMPLES
    precond = (query_sketch.astype(jnp.float32) / (math.sqrt(K) * (diag + DAMPING))).astype(jnp.bfloat16)
    raw_scores = jnp.dot(precond, sketch.T, preferred_element_type=jnp.float32)
    self_pair = query_ids[:, None] == example_ids.reshape(EXAMPLES)[None, :]
    scores = jnp.where(self_pair, jnp.float32(0.0), raw_scores).reshape(NQ, EXA, EXB)
    return (gram, scores)
```

```python
import functools
import math

import jax
import jax.numpy as jnp
from jax import lax
from jax.experimental import pallas as pl
from jax.experimental.pallas import tpu as pltpu
from jax.sharding import PartitionSpec as P

DAMPING = 0.1
ACT_CUTS = 2
GRAD_CUTS = 4
NT = (((1,), (1,)), ((), ()))


def partner(index, step, count):
    if count & (count - 1) == 0:
        return index ^ step
    return (index + step) % count


def source(index, step, count):
    if count & (count - 1) == 0:
        return index ^ step
    return lax.rem(index + count - step, count)


def exchange(block, axis, step):
    count = lax.axis_size(axis)
    return lax.ppermute(block, axis, [(i, partner(i, step, count)) for i in range(count)])


def sketch_kernel(
    acts_hbm, grads_hbm, act_proj_hbm, grad_proj_hbm, count_ref, out_ref,
    acts, grads, act_proj, grad_proj, turned, act_sems, grad_sems,
):
    seq_len = acts.shape[0]
    rank = act_proj.shape[0]

    def copies(source_hbm, target, sems, slot, cuts):
        width = target.shape[1] // cuts
        return [
            pltpu.make_async_copy(
                source_hbm.at[:, pl.ds(c * width, width)],
                target.at[:, pl.ds(c * width, width)],
                sems.at[slot, c],
            )
            for c in range(cuts)
        ]

    act_copies = list(
        zip(
            copies(act_proj_hbm, act_proj, act_sems, 0, ACT_CUTS),
            copies(acts_hbm, acts, act_sems, 1, ACT_CUTS),
        )
    )
    grad_copies = list(
        zip(
            copies(grad_proj_hbm, grad_proj, grad_sems, 0, GRAD_CUTS),
            copies(grads_hbm, grads, grad_sems, 1, GRAD_CUTS),
        )
    )
    for pair in act_copies + grad_copies:
        for copy in pair:
            copy.start()
    act_width = acts.shape[1] // ACT_CUTS
    act_sum = jnp.zeros((seq_len, rank), jnp.float32)
    for c, pair in enumerate(act_copies):
        for copy in pair:
            copy.wait()
        cols = pl.ds(c * act_width, act_width)
        act_sum += lax.dot_general(
            acts[:, cols], act_proj[:, cols], NT, preferred_element_type=jnp.float32
        )
    grad_width = grads.shape[1] // GRAD_CUTS
    grad_sum = jnp.zeros((rank, seq_len), jnp.float32)
    for c, pair in enumerate(grad_copies):
        for copy in pair:
            copy.wait()
        cols = pl.ds(c * grad_width, grad_width)
        grad_sum += lax.dot_general(
            grad_proj[:, cols], grads[:, cols], NT, preferred_element_type=jnp.float32
        )
    live = lax.broadcasted_iota(jnp.int32, (rank, seq_len), 1) < count_ref[0, 0]
    turned[...] = jnp.where(live, grad_sum, 0.0)
    act_low = act_sum.astype(jnp.bfloat16)
    halves = [
        jnp.dot(
            turned[pl.ds(side, rank // 2, stride=2), :].astype(jnp.bfloat16),
            act_low,
            preferred_element_type=jnp.float32,
        )
        for side in range(2)
    ]
    outer = jnp.concatenate(halves, axis=1) * (1.0 / math.sqrt(seq_len))
    out_ref[...] = outer.astype(jnp.bfloat16)


def make_sketch(acts, grads, act_proj, grad_proj, tok_count):
    seq_len, width = acts.shape
    hidden = grads.shape[1]
    rank = act_proj.shape[0]
    return pl.pallas_call(
        sketch_kernel,
        out_shape=jax.ShapeDtypeStruct((rank // 2, 2 * rank), jnp.bfloat16),
        in_specs=[pl.BlockSpec(memory_space=pl.ANY)] * 4
        + [pl.BlockSpec(memory_space=pltpu.SMEM)],
        out_specs=pl.BlockSpec(memory_space=pltpu.VMEM),
        scratch_shapes=[
            pltpu.VMEM((seq_len, width), jnp.bfloat16),
            pltpu.VMEM((seq_len, hidden), jnp.bfloat16),
            pltpu.VMEM((rank, width), jnp.bfloat16),
            pltpu.VMEM((rank, hidden), jnp.bfloat16),
            pltpu.VMEM((rank, seq_len), jnp.float32),
            pltpu.SemaphoreType.DMA((2, ACT_CUTS)),
            pltpu.SemaphoreType.DMA((2, GRAD_CUTS)),
        ],
        compiler_params=pltpu.CompilerParams(vmem_limit_bytes=16 * 2**20),
        name="sketch",
    )(acts, grads, act_proj, grad_proj, tok_count)


def place_rows(sizes, pieces, rows):
    ex_count, feat_count, pb_count = sizes
    ex, feat, pb = lax.axis_index("ex"), lax.axis_index("feat"), lax.axis_index("pb")
    for k in range(ex_count):
        for s in range(feat_count * pb_count):
            column = (
                source(feat, s // pb_count, feat_count) * pb_count
                + source(pb, s % pb_count, pb_count)
            )
            rows[column * ex_count + source(ex, k, ex_count)] = pieces[k][s].astype(jnp.float32)


def score_kernel(sizes, query_ref, *refs):
    ex_count, feat_count, pb_count = sizes
    pieces, refs = refs[:ex_count], refs[ex_count:]
    outs, (rows, scaled, result, chunks) = refs[:-4], refs[-4:]
    ex, feat, pb = lax.axis_index("ex"), lax.axis_index("feat"), lax.axis_index("pb")
    fp_count = feat_count * pb_count
    examples = ex_count * fp_count
    lines, lanes = rows.shape[1:]
    block_lines = lines // ex_count
    place_rows(sizes, pieces, rows)
    block = rows[:, pl.ds(ex * block_lines, block_lines), :]
    diag = jnp.sum(block * block, axis=0) / examples
    weight = 1.0 / (math.sqrt(lines * lanes) * (diag + DAMPING))
    scaled[...] = (block * weight[None]).reshape(examples * block_lines, lanes)
    parts = [scaled[pl.ds(j, examples, stride=block_lines), :] for j in range(block_lines)]
    wide = jnp.concatenate(parts, axis=1)
    high = wide.astype(jnp.bfloat16)
    low = (wide - high.astype(jnp.float32)).astype(jnp.bfloat16)
    both = jnp.concatenate([high, low], axis=0)
    products = lax.dot_general(both, query_ref[...], NT, preferred_element_type=jnp.float32)
    result[...] = (products[:examples] + products[examples:]).reshape(result.shape)
    width = query_ref.shape[0] // (ex_count // pb_count)
    for t in range(ex_count):
        column = feat * pb_count + t % pb_count
        chunks[t] = result[column, :, pl.ds((t // pb_count) * width, width)]
    for j in range(ex_count):
        outs[j][...] = chunks[partner(ex, j, ex_count)]


def partial_scores(sizes, queries, pieces):
    ex_count, feat_count, pb_count = sizes
    examples = ex_count * feat_count * pb_count
    lines, lanes = pieces[0].shape[1:]
    chunk = (ex_count, queries.shape[0] * pb_count // ex_count)
    vmem = pl.BlockSpec(memory_space=pltpu.VMEM)
    return pl.pallas_call(
        functools.partial(score_kernel, sizes),
        out_shape=[jax.ShapeDtypeStruct(chunk, jnp.float32)] * ex_count,
        in_specs=[vmem] * (1 + ex_count),
        out_specs=[vmem] * ex_count,
        scratch_shapes=[
            pltpu.VMEM((examples, lines, lanes), jnp.float32),
            pltpu.VMEM((examples * (lines // ex_count), lanes), jnp.float32),
            pltpu.VMEM((feat_count * pb_count, ex_count, queries.shape[0]), jnp.float32),
            pltpu.VMEM((ex_count, *chunk), jnp.float32),
        ],
        compiler_params=pltpu.CompilerParams(vmem_limit_bytes=24 * 2**20),
        name="scores",
    )(queries, *pieces)


def gram_kernel(sizes, *refs):
    ex_count, feat_count, pb_count = sizes
    pieces, (out_ref, rows, left, right) = refs[:ex_count], refs[ex_count:]
    ex = lax.axis_index("ex")
    fp_count = feat_count * pb_count
    examples = ex_count * fp_count
    lines, lanes = rows.shape[1:]
    left_lines, right_lines = lines // ex_count, lines // fp_count

    @pl.when(pl.program_id(0) == 0)
    def _():
        fp = lax.axis_index("feat") * pb_count + lax.axis_index("pb")
        place_rows(sizes, pieces, rows)
        left_block = rows[:, pl.ds(ex * left_lines, left_lines), :]
        left[...] = left_block.reshape(examples * left_lines, lanes)
        right_block = rows[:, pl.ds(fp * right_lines, right_lines), :]
        right[...] = right_block.reshape(examples * right_lines, lanes)

    here = left[pl.ds(pl.program_id(0), examples, stride=left_lines), :].T.astype(jnp.bfloat16)
    across = jnp.concatenate(
        [right[pl.ds(j, examples, stride=right_lines), :] for j in range(right_lines)], axis=1
    ).astype(jnp.bfloat16)
    out_ref[...] = jnp.dot(here, across, preferred_element_type=jnp.float32) * (1.0 / examples)


def make_gram(sizes, pieces):
    ex_count, feat_count, pb_count = sizes
    fp_count = feat_count * pb_count
    examples = ex_count * fp_count
    lines, lanes = pieces[0].shape[1:]
    left_lines, right_lines = lines // ex_count, lines // fp_count
    whole = pl.BlockSpec(memory_space=pltpu.VMEM)
    return pl.pallas_call(
        functools.partial(gram_kernel, sizes),
        grid=(left_lines,),
        out_shape=jax.ShapeDtypeStruct((left_lines * lanes, right_lines * lanes), jnp.float32),
        in_specs=[whole] * ex_count,
        out_specs=pl.BlockSpec((lanes, right_lines * lanes), lambda i: (i, 0)),
        scratch_shapes=[
            pltpu.VMEM((examples, lines, lanes), jnp.float32),
            pltpu.VMEM((examples * left_lines, lanes), jnp.float32),
            pltpu.VMEM((examples * right_lines, lanes), jnp.float32),
        ],
        compiler_params=pltpu.CompilerParams(vmem_limit_bytes=24 * 2**20),
        cost_estimate=pl.CostEstimate(
            flops=2 * 256 * left_lines * lanes * right_lines * lanes,
            bytes_accessed=4 * left_lines * lanes * right_lines * lanes,
            transcendentals=0,
        ),
        name="gram",
    )(*pieces)


def shards(
    activations, out_grads, act_proj, grad_proj, tok_counts, example_ids, query_sketch, query_ids
):
    ex_count, feat_count, pb_count = (lax.axis_size(axis) for axis in ("ex", "feat", "pb"))
    sizes = (ex_count, feat_count, pb_count)
    sketch = make_sketch(
        activations[0, 0], out_grads[0, 0], act_proj.T, grad_proj.T, tok_counts
    )
    block = sketch[None]
    for axis, count in (("pb", pb_count), ("feat", feat_count)):
        block = jnp.concatenate([block] + [exchange(block, axis, k) for k in range(1, count)])
    pieces = [block] + [exchange(block, "ex", k) for k in range(1, ex_count)]
    chunks = partial_scores(sizes, query_sketch, pieces)
    half = ex_count // pb_count
    arrived = [
        lax.ppermute(
            chunk,
            ("ex", "pb"),
            [
                (
                    e * pb_count + p,
                    (p * half + partner(e, j, ex_count) // pb_count) * pb_count
                    + partner(e, j, ex_count) % pb_count,
                )
                for e in range(ex_count)
                for p in range(pb_count)
            ],
        )
        for j, chunk in enumerate(chunks)
    ]
    gram = make_gram(sizes, pieces)
    width = query_ids.shape[0] // ex_count
    query_here = lax.dynamic_slice_in_dim(query_ids, lax.axis_index("ex") * width, width, 0)
    self_pair = example_ids == query_here[None, :]
    scores = jnp.where(self_pair, jnp.float32(0.0), sum(arrived))
    return gram, scores.T[:, :, None]


def solution(mesh):
    return jax.shard_map(
        shards,
        mesh=mesh,
        in_specs=(
            P(("groups", "ex"), ("feat", "pb"), None, None),
            P(("groups", "ex"), ("feat", "pb"), None, None),
            P(),
            P(),
            P(("groups", "ex"), ("feat", "pb")),
            P("groups", ("feat", "pb")),
            P(("groups", "pb"), "ex"),
            P("groups"),
        ),
        out_specs=(P(("groups", "ex"), ("feat", "pb")), P(("groups", "ex"), None, ("feat", "pb"))),
        check_vma=False,
    )
```

```python
import functools
import math

import jax
import jax.numpy as jnp
from jax import lax
from jax.experimental import pallas as pl
from jax.experimental.pallas import tpu as pltpu
from jax.sharding import PartitionSpec as P

DAMPING = 0.1
ACT_CUTS = 2
GRAD_CUTS = 4
NT = (((1,), (1,)), ((), ()))


def exchange(block, axis, step):
    return lax.ppermute(block, axis, [(i, i ^ step) for i in range(lax.axis_size(axis))])


def sketch_kernel(
    acts_hbm, grads_hbm, act_proj_hbm, grad_proj_hbm, count_ref, out_ref,
    acts, grads, act_proj, grad_proj, turned, act_sems, grad_sems,
):
    seq_len = acts.shape[0]
    rank = act_proj.shape[0]

    def copies(source_hbm, target, sems, slot, cuts):
        width = target.shape[1] // cuts
        return [
            pltpu.make_async_copy(
                source_hbm.at[:, pl.ds(c * width, width)],
                target.at[:, pl.ds(c * width, width)],
                sems.at[slot, c],
            )
            for c in range(cuts)
        ]

    act_copies = list(
        zip(
            copies(act_proj_hbm, act_proj, act_sems, 0, ACT_CUTS),
            copies(acts_hbm, acts, act_sems, 1, ACT_CUTS),
        )
    )
    grad_copies = list(
        zip(
            copies(grad_proj_hbm, grad_proj, grad_sems, 0, GRAD_CUTS),
            copies(grads_hbm, grads, grad_sems, 1, GRAD_CUTS),
        )
    )
    for pair in act_copies + grad_copies:
        for copy in pair:
            copy.start()
    act_width = acts.shape[1] // ACT_CUTS
    act_sum = jnp.zeros((seq_len, rank), jnp.float32)
    for c, pair in enumerate(act_copies):
        for copy in pair:
            copy.wait()
        cols = pl.ds(c * act_width, act_width)
        act_sum += lax.dot_general(
            acts[:, cols], act_proj[:, cols], NT, preferred_element_type=jnp.float32
        )
    grad_width = grads.shape[1] // GRAD_CUTS
    grad_sum = jnp.zeros((rank, seq_len), jnp.float32)
    for c, pair in enumerate(grad_copies):
        for copy in pair:
            copy.wait()
        cols = pl.ds(c * grad_width, grad_width)
        grad_sum += lax.dot_general(
            grad_proj[:, cols], grads[:, cols], NT, preferred_element_type=jnp.float32
        )
    live = lax.broadcasted_iota(jnp.int32, (rank, seq_len), 1) < count_ref[...]
    turned[...] = jnp.where(live, grad_sum, 0.0)
    act_low = act_sum.astype(jnp.bfloat16)
    halves = [
        jnp.dot(
            turned[pl.ds(side, rank // 2, stride=2), :].astype(jnp.bfloat16),
            act_low,
            preferred_element_type=jnp.float32,
        )
        for side in range(2)
    ]
    outer = jnp.concatenate(halves, axis=1) * (1.0 / math.sqrt(seq_len))
    out_ref[...] = outer.astype(jnp.bfloat16)


def make_sketch(acts, grads, act_proj, grad_proj, tok_count):
    seq_len, width = acts.shape
    hidden = grads.shape[1]
    rank = act_proj.shape[0]
    return pl.pallas_call(
        sketch_kernel,
        out_shape=jax.ShapeDtypeStruct((rank // 2, 2 * rank), jnp.bfloat16),
        in_specs=[pl.BlockSpec(memory_space=pl.ANY)] * 4
        + [pl.BlockSpec(memory_space=pltpu.VMEM)],
        out_specs=pl.BlockSpec(memory_space=pltpu.VMEM),
        scratch_shapes=[
            pltpu.VMEM((seq_len, width), jnp.bfloat16),
            pltpu.VMEM((seq_len, hidden), jnp.bfloat16),
            pltpu.VMEM((rank, width), jnp.bfloat16),
            pltpu.VMEM((rank, hidden), jnp.bfloat16),
            pltpu.VMEM((rank, seq_len), jnp.float32),
            pltpu.SemaphoreType.DMA((2, ACT_CUTS)),
            pltpu.SemaphoreType.DMA((2, GRAD_CUTS)),
        ],
        compiler_params=pltpu.CompilerParams(vmem_limit_bytes=60 * 2**20),
        name="sketch",
    )(acts, grads, act_proj, grad_proj, tok_count)


def place_rows(sizes, pieces, rows):
    ex_count, fp_count = sizes[0], sizes[1] * sizes[2]
    ex = lax.axis_index("ex")
    fp = lax.axis_index("feat") * sizes[2] + lax.axis_index("pb")
    for k in range(ex_count):
        for s in range(fp_count):
            rows[(fp ^ s) * ex_count + (ex ^ k)] = pieces[k][s].astype(jnp.float32)


def score_kernel(sizes, query_ref, *refs):
    ex_count, feat_count, pb_count = sizes
    half = ex_count // pb_count
    pieces, outs = refs[:ex_count], refs[ex_count : ex_count + half]
    rows, scaled, chunks = refs[-3:]
    ex, feat = lax.axis_index("ex"), lax.axis_index("feat")
    examples, lines, lanes = rows.shape
    block_lines = lines // ex_count
    mine = ex_count * pb_count
    place_rows(sizes, pieces, rows)
    block = rows[:, pl.ds(ex * block_lines, block_lines), :]
    diag = jnp.sum(block * block, axis=0) / examples
    weight = 1.0 / (math.sqrt(lines * lanes) * (diag + DAMPING))
    own = rows[pl.ds(feat * mine, mine), pl.ds(ex * block_lines, block_lines), :]
    scaled[...] = (own * weight[None]).reshape(mine * block_lines, lanes)
    parts = [scaled[pl.ds(j, mine, stride=block_lines), :] for j in range(block_lines)]
    wide = jnp.concatenate(parts, axis=1)
    high = wide.astype(jnp.bfloat16)
    low = (wide - high.astype(jnp.float32)).astype(jnp.bfloat16)
    both = jnp.concatenate([high, low], axis=0)
    products = lax.dot_general(both, query_ref[...], NT, preferred_element_type=jnp.float32)
    result = products[:mine] + products[mine:]
    width = chunks.shape[2]
    for t in range(half):
        chunks[t] = result[:, t * width : (t + 1) * width]
    for i in range(half):
        outs[i][...] = chunks[lax.rem(ex, half) ^ i]


def partial_scores(sizes, queries, pieces):
    ex_count, feat_count, pb_count = sizes
    examples = ex_count * feat_count * pb_count
    lines, lanes = pieces[0].shape[1:]
    half = ex_count // pb_count
    chunk = (pb_count * ex_count, queries.shape[0] // half)
    vmem = pl.BlockSpec(memory_space=pltpu.VMEM)
    return pl.pallas_call(
        functools.partial(score_kernel, sizes),
        out_shape=[jax.ShapeDtypeStruct(chunk, jnp.float32)] * half,
        in_specs=[vmem] * (1 + ex_count),
        out_specs=[vmem] * half,
        scratch_shapes=[
            pltpu.VMEM((examples, lines, lanes), jnp.float32),
            pltpu.VMEM((pb_count * lines, lanes), jnp.float32),
            pltpu.VMEM((half, *chunk), jnp.float32),
        ],
        compiler_params=pltpu.CompilerParams(vmem_limit_bytes=24 * 2**20),
        name="scores",
    )(queries, *pieces)


def gram_kernel(sizes, *refs):
    ex_count, fp_count = sizes[0], sizes[1] * sizes[2]
    pieces, (out_hbm, rows, left, right, result, sems) = refs[:ex_count], refs[ex_count:]
    ex = lax.axis_index("ex")
    fp = lax.axis_index("feat") * sizes[2] + lax.axis_index("pb")
    examples, lines, lanes = rows.shape
    left_lines, right_lines = lines // ex_count, lines // fp_count
    place_rows(sizes, pieces, rows)
    block = rows[:, pl.ds(ex * left_lines, left_lines), :]
    left[...] = block.reshape(examples * left_lines, lanes)
    block = rows[:, pl.ds(fp * right_lines, right_lines), :]
    right[...] = block.reshape(examples * right_lines, lanes)
    across = jnp.concatenate(
        [right[pl.ds(j, examples, stride=right_lines), :] for j in range(right_lines)], axis=1
    ).astype(jnp.bfloat16)
    copies = []
    for i in range(left_lines):
        here = left[pl.ds(i, examples, stride=left_lines), :].T.astype(jnp.bfloat16)
        band = pl.ds(i * lanes, lanes)
        total = jnp.dot(here, across, preferred_element_type=jnp.float32)
        result[band, :] = total * (1.0 / examples)
        copies.append(
            pltpu.make_async_copy(result.at[band, :], out_hbm.at[band, :], sems.at[i])
        )
        copies[-1].start()
    for copy in copies:
        copy.wait()


def make_gram(sizes, pieces):
    ex_count, fp_count = sizes[0], sizes[1] * sizes[2]
    examples = ex_count * fp_count
    lines, lanes = pieces[0].shape[1:]
    left_lines, right_lines = lines // ex_count, lines // fp_count
    shape = (left_lines * lanes, right_lines * lanes)
    return pl.pallas_call(
        functools.partial(gram_kernel, sizes),
        out_shape=jax.ShapeDtypeStruct(shape, jnp.float32),
        in_specs=[pl.BlockSpec(memory_space=pltpu.VMEM)] * ex_count,
        out_specs=pl.BlockSpec(memory_space=pl.ANY),
        scratch_shapes=[
            pltpu.VMEM((examples, lines, lanes), jnp.float32),
            pltpu.VMEM((examples * left_lines, lanes), jnp.float32),
            pltpu.VMEM((examples * right_lines, lanes), jnp.float32),
            pltpu.VMEM(shape, jnp.float32),
            pltpu.SemaphoreType.DMA((left_lines,)),
        ],
        compiler_params=pltpu.CompilerParams(vmem_limit_bytes=24 * 2**20),
        cost_estimate=pl.CostEstimate(
            flops=2 * 256 * shape[0] * shape[1],
            bytes_accessed=4 * shape[0] * shape[1],
            transcendentals=0,
        ),
        name="gram",
    )(*pieces)


def to_owners(chunks, ex_count, pb_count):
    half = ex_count // pb_count
    pairs = [
        [
            (e * pb_count + p, (e ^ (((e // half) ^ p) * half + i)) * pb_count + e // half)
            for e in range(ex_count)
            for p in range(pb_count)
        ]
        for i in range(half)
    ]
    return sum(lax.ppermute(chunk, ("ex", "pb"), pairs[i]) for i, chunk in enumerate(chunks))


def shards(
    activations, out_grads, act_proj, grad_proj, tok_counts, example_ids, query_sketch, query_ids
):
    ex_count, feat_count, pb_count = (lax.axis_size(axis) for axis in ("ex", "feat", "pb"))
    sizes = (ex_count, feat_count, pb_count)
    sketch = make_sketch(
        activations[0, 0], out_grads[0, 0], act_proj.T, grad_proj.T, tok_counts
    )
    block = sketch[None]
    for axis, count in (("pb", pb_count), ("feat", feat_count)):
        block = jnp.concatenate([block] + [exchange(block, axis, k) for k in range(1, count)])
    pieces = [block] + [exchange(block, "ex", k) for k in range(1, ex_count)]
    part = to_owners(partial_scores(sizes, query_sketch, pieces), ex_count, pb_count)
    gram = make_gram(sizes, pieces)
    part = part.reshape(pb_count, ex_count, -1)
    pb = lax.axis_index("pb")
    total = lax.dynamic_index_in_dim(part, pb, 0, keepdims=False)
    for k in range(1, pb_count):
        theirs = lax.dynamic_index_in_dim(part, pb ^ k, 0, keepdims=False)
        total += exchange(theirs, "pb", k)
    width = query_ids.shape[0] // ex_count
    query_here = lax.dynamic_slice_in_dim(query_ids, lax.axis_index("ex") * width, width, 0)
    self_pair = example_ids == query_here[None, :]
    scores = jnp.where(self_pair, jnp.float32(0.0), total)
    return gram, scores.T[:, :, None]


def solution(mesh):
    return jax.shard_map(
        shards,
        mesh=mesh,
        in_specs=(
            P(("groups", "ex"), ("feat", "pb"), None, None),
            P(("groups", "ex"), ("feat", "pb"), None, None),
            P(),
            P(),
            P(("groups", "ex"), ("feat", "pb")),
            P("groups", ("feat", "pb")),
            P(("groups", "pb"), "ex"),
            P("groups"),
        ),
        out_specs=(P(("groups", "ex"), ("feat", "pb")), P(("groups", "ex"), None, ("feat", "pb"))),
        check_vma=False,
    )
```

```python
import functools
import math

import jax
import jax.numpy as jnp
from jax import lax
from jax.experimental import pallas as pl
from jax.experimental.pallas import tpu as pltpu
from jax.sharding import PartitionSpec as P

DAMPING = 0.1
ACT_CUTS = 2
GRAD_CUTS = 4
NT = (((1,), (1,)), ((), ()))


def exchange(block, axis, step):
    return lax.ppermute(block, axis, [(i, i ^ step) for i in range(lax.axis_size(axis))])


def sketch_kernel(
    acts_hbm, grads_hbm, act_proj_hbm, grad_proj_hbm, count_ref, out_ref,
    acts, grads, act_proj, grad_proj, turned, act_sems, grad_sems,
):
    seq_len = acts.shape[0]
    rank = act_proj.shape[0]

    def copies(source_hbm, target, sems, slot, cuts):
        width = target.shape[1] // cuts
        return [
            pltpu.make_async_copy(
                source_hbm.at[:, pl.ds(c * width, width)],
                target.at[:, pl.ds(c * width, width)],
                sems.at[slot, c],
            )
            for c in range(cuts)
        ]

    act_copies = list(
        zip(
            copies(act_proj_hbm, act_proj, act_sems, 0, ACT_CUTS),
            copies(acts_hbm, acts, act_sems, 1, ACT_CUTS),
        )
    )
    grad_copies = list(
        zip(
            copies(grad_proj_hbm, grad_proj, grad_sems, 0, GRAD_CUTS),
            copies(grads_hbm, grads, grad_sems, 1, GRAD_CUTS),
        )
    )
    for pair in act_copies + grad_copies:
        for copy in pair:
            copy.start()
    act_width = acts.shape[1] // ACT_CUTS
    act_sum = jnp.zeros((seq_len, rank), jnp.float32)
    for c, pair in enumerate(act_copies):
        for copy in pair:
            copy.wait()
        cols = pl.ds(c * act_width, act_width)
        act_sum += lax.dot_general(
            acts[:, cols], act_proj[:, cols], NT, preferred_element_type=jnp.float32
        )
    grad_width = grads.shape[1] // GRAD_CUTS
    grad_sum = jnp.zeros((rank, seq_len), jnp.float32)
    for c, pair in enumerate(grad_copies):
        for copy in pair:
            copy.wait()
        cols = pl.ds(c * grad_width, grad_width)
        grad_sum += lax.dot_general(
            grad_proj[:, cols], grads[:, cols], NT, preferred_element_type=jnp.float32
        )
    live = lax.broadcasted_iota(jnp.int32, (rank, seq_len), 1) < count_ref[...]
    turned[...] = jnp.where(live, grad_sum, 0.0)
    act_low = act_sum.astype(jnp.bfloat16)
    halves = [
        jnp.dot(
            turned[pl.ds(side, rank // 2, stride=2), :].astype(jnp.bfloat16),
            act_low,
            preferred_element_type=jnp.float32,
        )
        for side in range(2)
    ]
    outer = jnp.concatenate(halves, axis=1) * (1.0 / math.sqrt(seq_len))
    out_ref[...] = outer.astype(jnp.bfloat16)


def make_sketch(acts, grads, act_proj, grad_proj, tok_count):
    seq_len, width = acts.shape
    hidden = grads.shape[1]
    rank = act_proj.shape[0]
    return pl.pallas_call(
        sketch_kernel,
        out_shape=jax.ShapeDtypeStruct((rank // 2, 2 * rank), jnp.bfloat16),
        in_specs=[pl.BlockSpec(memory_space=pl.ANY)] * 4
        + [pl.BlockSpec(memory_space=pltpu.VMEM)],
        out_specs=pl.BlockSpec(memory_space=pltpu.VMEM),
        scratch_shapes=[
            pltpu.VMEM((seq_len, width), jnp.bfloat16),
            pltpu.VMEM((seq_len, hidden), jnp.bfloat16),
            pltpu.VMEM((rank, width), jnp.bfloat16),
            pltpu.VMEM((rank, hidden), jnp.bfloat16),
            pltpu.VMEM((rank, seq_len), jnp.float32),
            pltpu.SemaphoreType.DMA((2, ACT_CUTS)),
            pltpu.SemaphoreType.DMA((2, GRAD_CUTS)),
        ],
        compiler_params=pltpu.CompilerParams(vmem_limit_bytes=60 * 2**20),
        name="sketch",
    )(acts, grads, act_proj, grad_proj, tok_count)


def spread(block, distances):
    pairs = [
        (e * len(distances) + p, (e ^ k) * len(distances) + p)
        for e in range(lax.axis_size("ex"))
        for p, k in enumerate(distances)
    ]
    return lax.ppermute(block, ("ex", "pb"), pairs)


def gather_rows(sketch):
    ex_count = lax.axis_size("ex")
    fp_count = lax.axis_size(("feat", "pb"))
    own = sketch[None]
    block = jnp.concatenate([own] + [exchange(own, ("feat", "pb"), s) for s in range(1, fp_count)])
    pieces = [(block, (0, 0), 0)]
    for k in range(1, ex_count, 2):
        distances = (k, min(k + 1, ex_count - 1))
        near = spread(block, distances)
        pieces.append((near, distances, 0))
        if distances[0] != distances[1]:
            pieces.append((exchange(near, "pb", 1), distances, 1))
    return pieces


def place_rows(sizes, sources, pieces, rows):
    ex_count, fp_count = sizes[0], sizes[1] * sizes[2]
    ex, pb = lax.axis_index("ex"), lax.axis_index("pb")
    fp = lax.axis_index("feat") * sizes[2] + pb
    for piece, (distances, core) in zip(pieces, sources):
        first, step = distances[core], distances[1 - core] - distances[core]
        where = ex ^ (first + step * pb)
        for s in range(fp_count):
            rows[(fp ^ core ^ s) * ex_count + where] = piece[s].astype(jnp.float32)


def score_kernel(sizes, sources, query_ref, *refs):
    ex_count, feat_count, pb_count = sizes
    half = ex_count // pb_count
    pieces, outs = refs[: len(sources)], refs[len(sources) : len(sources) + half]
    own_ref, rows, scaled, chunks = refs[-4:]
    ex, feat = lax.axis_index("ex"), lax.axis_index("feat")
    near = lax.div(ex, half) == lax.axis_index("pb")
    here = lax.rem(ex, half)
    examples, lines, lanes = rows.shape
    block_lines = lines // ex_count
    mine = ex_count * pb_count
    place_rows(sizes, sources, pieces, rows)
    block = rows[:, pl.ds(ex * block_lines, block_lines), :]
    diag = jnp.sum(block * block, axis=0) / examples
    weight = 1.0 / (math.sqrt(lines * lanes) * (diag + DAMPING))
    own = rows[pl.ds(feat * mine, mine), pl.ds(ex * block_lines, block_lines), :]
    scaled[...] = (own * weight[None]).reshape(mine * block_lines, lanes)
    parts = [scaled[pl.ds(j, mine, stride=block_lines), :] for j in range(block_lines)]
    wide = jnp.concatenate(parts, axis=1)
    high = wide.astype(jnp.bfloat16)
    low = (wide - high.astype(jnp.float32)).astype(jnp.bfloat16)
    both = jnp.concatenate([high, low], axis=0)
    products = lax.dot_general(both, query_ref[...], NT, preferred_element_type=jnp.float32)
    result = products[:mine] + products[mine:]
    width = chunks.shape[2]
    for t in range(half):
        chunks[t] = result[:, t * width : (t + 1) * width]
    shift = near.astype(jnp.int32)
    for i in range(half - 1):
        outs[i][...] = chunks[here ^ (i + shift)]
    outs[half - 1][...] = jnp.where(near, 0.0, chunks[here ^ (half - 1)])
    own_ref[...] = jnp.where(near, chunks[here], 0.0)


def partial_scores(sizes, queries, pieces):
    ex_count, feat_count, pb_count = sizes
    examples = ex_count * feat_count * pb_count
    lines, lanes = pieces[0][0].shape[1:]
    half = ex_count // pb_count
    chunk = (pb_count * ex_count, queries.shape[0] // half)
    vmem = pl.BlockSpec(memory_space=pltpu.VMEM)
    return pl.pallas_call(
        functools.partial(score_kernel, sizes, [piece[1:] for piece in pieces]),
        out_shape=[jax.ShapeDtypeStruct(chunk, jnp.float32)] * (half + 1),
        in_specs=[vmem] * (1 + len(pieces)),
        out_specs=[vmem] * (half + 1),
        scratch_shapes=[
            pltpu.VMEM((examples, lines, lanes), jnp.float32),
            pltpu.VMEM((pb_count * lines, lanes), jnp.float32),
            pltpu.VMEM((half, *chunk), jnp.float32),
        ],
        compiler_params=pltpu.CompilerParams(vmem_limit_bytes=24 * 2**20),
        name="scores",
    )(queries, *[piece[0] for piece in pieces])


def gram_kernel(sizes, sources, kept_ref, *refs):
    ex_count, fp_count = sizes[0], sizes[1] * sizes[2]
    pieces = refs[: len(sources)]
    out_hbm, kept_out_ref, rows, left, right, result, sems = refs[len(sources) :]
    ex = lax.axis_index("ex")
    fp = lax.axis_index("feat") * sizes[2] + lax.axis_index("pb")
    examples, lines, lanes = rows.shape
    left_lines, right_lines = lines // ex_count, lines // fp_count
    kept_out_ref[...] = kept_ref[...]
    place_rows(sizes, sources, pieces, rows)
    block = rows[:, pl.ds(ex * left_lines, left_lines), :]
    left[...] = block.reshape(examples * left_lines, lanes)
    block = rows[:, pl.ds(fp * right_lines, right_lines), :]
    right[...] = block.reshape(examples * right_lines, lanes)
    across = jnp.concatenate(
        [right[pl.ds(j, examples, stride=right_lines), :] for j in range(right_lines)], axis=1
    ).astype(jnp.bfloat16)
    copies = []
    for i in range(left_lines):
        here = left[pl.ds(i, examples, stride=left_lines), :].T.astype(jnp.bfloat16)
        band = pl.ds(i * lanes, lanes)
        total = jnp.dot(here, across, preferred_element_type=jnp.float32)
        result[band, :] = total * (1.0 / examples)
        copies.append(
            pltpu.make_async_copy(result.at[band, :], out_hbm.at[band, :], sems.at[i])
        )
        copies[-1].start()
    for copy in copies:
        copy.wait()


def make_gram(sizes, pieces, kept):
    ex_count, fp_count = sizes[0], sizes[1] * sizes[2]
    examples = ex_count * fp_count
    lines, lanes = pieces[0][0].shape[1:]
    left_lines, right_lines = lines // ex_count, lines // fp_count
    shape = (left_lines * lanes, right_lines * lanes)
    return pl.pallas_call(
        functools.partial(gram_kernel, sizes, [piece[1:] for piece in pieces]),
        out_shape=[
            jax.ShapeDtypeStruct(shape, jnp.float32),
            jax.ShapeDtypeStruct(kept.shape, kept.dtype),
        ],
        in_specs=[pl.BlockSpec(memory_space=pltpu.VMEM)] * (1 + len(pieces)),
        out_specs=[pl.BlockSpec(memory_space=pl.ANY), pl.BlockSpec(memory_space=pltpu.VMEM)],
        scratch_shapes=[
            pltpu.VMEM((examples, lines, lanes), jnp.float32),
            pltpu.VMEM((examples * left_lines, lanes), jnp.float32),
            pltpu.VMEM((examples * right_lines, lanes), jnp.float32),
            pltpu.VMEM(shape, jnp.float32),
            pltpu.SemaphoreType.DMA((left_lines,)),
        ],
        compiler_params=pltpu.CompilerParams(vmem_limit_bytes=24 * 2**20),
        cost_estimate=pl.CostEstimate(
            flops=2 * 256 * shape[0] * shape[1],
            bytes_accessed=4 * shape[0] * shape[1],
            transcendentals=0,
        ),
        name="gram",
    )(kept, *[piece[0] for piece in pieces])


def to_owners(chunks, ex_count):
    half = ex_count // 2
    arrived = []
    for i, chunk in enumerate(chunks):
        pairs = []
        for e in range(ex_count):
            near, far = e // half, 1 - e // half
            pairs.append((e * 2 + near, (e ^ (i + 1 if i < half - 1 else 1)) * 2 + near))
            pairs.append((e * 2 + far, (e ^ (half + i)) * 2 + near))
        arrived.append(lax.ppermute(chunk, ("ex", "pb"), pairs))
    return sum(arrived)


def shards(
    activations, out_grads, act_proj, grad_proj, tok_counts, example_ids, query_sketch, query_ids
):
    ex_count, feat_count, pb_count = (lax.axis_size(axis) for axis in ("ex", "feat", "pb"))
    sizes = (ex_count, feat_count, pb_count)
    sketch = make_sketch(
        activations[0, 0], out_grads[0, 0], act_proj.T, grad_proj.T, tok_counts
    )
    pieces = gather_rows(sketch)
    *chunks, own = partial_scores(sizes, query_sketch, pieces)
    part = to_owners(chunks, ex_count)
    gram, own = make_gram(sizes, pieces, own)
    part = (part + own).reshape(pb_count, ex_count, -1)
    pb = lax.axis_index("pb")
    theirs = lax.dynamic_index_in_dim(part, 1 - pb, 0, keepdims=False)
    total = lax.dynamic_index_in_dim(part, pb, 0, keepdims=False) + exchange(theirs, "pb", 1)
    width = query_ids.shape[0] // ex_count
    query_here = lax.dynamic_slice_in_dim(query_ids, lax.axis_index("ex") * width, width, 0)
    self_pair = example_ids == query_here[None, :]
    scores = jnp.where(self_pair, jnp.float32(0.0), total)
    return gram, scores.T[:, :, None]


def solution(mesh):
    return jax.shard_map(
        shards,
        mesh=mesh,
        in_specs=(
            P(("groups", "ex"), ("feat", "pb"), None, None),
            P(("groups", "ex"), ("feat", "pb"), None, None),
            P(),
            P(),
            P(("groups", "ex"), ("feat", "pb")),
            P("groups", ("feat", "pb")),
            P(("groups", "pb"), "ex"),
            P("groups"),
        ),
        out_specs=(P(("groups", "ex"), ("feat", "pb")), P(("groups", "ex"), None, ("feat", "pb"))),
        check_vma=False,
    )
```

```python
import functools
import math

import jax
import jax.numpy as jnp
from jax import lax
from jax.experimental import pallas as pl
from jax.experimental.pallas import tpu as pltpu
from jax.sharding import PartitionSpec as P

DAMPING = 0.1
NT = (((1,), (1,)), ((), ()))


def exchange(block, axis, step):
    return lax.ppermute(block, axis, [(i, i ^ step) for i in range(lax.axis_size(axis))])


def make_sketch(acts, grads, act_proj, grad_proj, tok_count):
    seq_len, rank = acts.shape[0], act_proj.shape[1]
    act_low = jnp.dot(acts, act_proj, preferred_element_type=jnp.float32).astype(jnp.bfloat16)
    grad_low = jnp.dot(grads, grad_proj, preferred_element_type=jnp.float32).astype(jnp.bfloat16)
    keep_mask = (jnp.arange(seq_len, dtype=jnp.int32) < tok_count).astype(jnp.bfloat16)
    kept = grad_low * keep_mask[:, None]
    outer_sum = jnp.dot(kept.T, act_low, preferred_element_type=jnp.float32) * (
        1.0 / math.sqrt(seq_len)
    )
    return outer_sum.astype(jnp.bfloat16).reshape(rank // 2, 2 * rank)


def spread(block, distances):
    pairs = [
        (e * len(distances) + p, (e ^ k) * len(distances) + p)
        for e in range(lax.axis_size("ex"))
        for p, k in enumerate(distances)
    ]
    return lax.ppermute(block, ("ex", "pb"), pairs)


def gather_rows(sketch):
    ex_count = lax.axis_size("ex")
    fp_count = lax.axis_size(("feat", "pb"))
    own = sketch[None]
    block = jnp.concatenate([own] + [exchange(own, ("feat", "pb"), s) for s in range(1, fp_count)])
    pieces = [(block, (0, 0), 0)]
    for k in range(1, ex_count, 2):
        distances = (k, min(k + 1, ex_count - 1))
        near = spread(block, distances)
        pieces.append((near, distances, 0))
        if distances[0] != distances[1]:
            pieces.append((exchange(near, "pb", 1), distances, 1))
    return pieces


def place_rows(sizes, sources, pieces, rows):
    ex_count, fp_count = sizes[0], sizes[1] * sizes[2]
    ex, pb = lax.axis_index("ex"), lax.axis_index("pb")
    fp = lax.axis_index("feat") * sizes[2] + pb
    for piece, (distances, core) in zip(pieces, sources):
        first, step = distances[core], distances[1 - core] - distances[core]
        where = ex ^ (first + step * pb)
        for s in range(fp_count):
            rows[(fp ^ core ^ s) * ex_count + where] = piece[s].astype(jnp.float32)


def score_kernel(sizes, sources, query_ref, query_ids_ref, example_ids_ref, *refs):
    ex_count, feat_count, pb_count = sizes
    half = ex_count // pb_count
    pieces, outs = refs[: len(sources)], refs[len(sources) : len(sources) + half]
    own_ref, open_ref, rows, scaled, chunks = refs[-5:]
    ex, feat = lax.axis_index("ex"), lax.axis_index("feat")
    near = lax.div(ex, half) == lax.axis_index("pb")
    here = lax.rem(ex, half)
    examples, lines, lanes = rows.shape
    block_lines = lines // ex_count
    mine = ex_count * pb_count
    place_rows(sizes, sources, pieces, rows)
    block = rows[:, pl.ds(ex * block_lines, block_lines), :]
    diag = jnp.sum(block * block, axis=0) / examples
    weight = 1.0 / (math.sqrt(lines * lanes) * (diag + DAMPING))
    own = rows[pl.ds(feat * mine, mine), pl.ds(ex * block_lines, block_lines), :]
    scaled[...] = (own * weight[None]).reshape(mine * block_lines, lanes)
    parts = [scaled[pl.ds(j, mine, stride=block_lines), :] for j in range(block_lines)]
    wide = jnp.concatenate(parts, axis=1)
    high = wide.astype(jnp.bfloat16)
    low = (wide - high.astype(jnp.float32)).astype(jnp.bfloat16)
    both = jnp.concatenate([high, low], axis=0)
    products = lax.dot_general(both, query_ref[...], NT, preferred_element_type=jnp.float32)
    result = products[:mine] + products[mine:]
    width = chunks.shape[2]
    for t in range(half):
        chunks[t] = result[:, t * width : (t + 1) * width]
    shift = near.astype(jnp.int32)
    for i in range(half - 1):
        outs[i][...] = chunks[here ^ (i + shift)]
    outs[half - 1][...] = jnp.where(near, 0.0, chunks[here ^ (half - 1)])
    own_ref[...] = jnp.where(near, chunks[here], 0.0)
    open_ref[...] = jnp.where(example_ids_ref[...] == query_ids_ref[...], 0.0, 1.0)


def partial_scores(sizes, queries, query_ids, example_ids, pieces):
    ex_count, feat_count, pb_count = sizes
    examples = ex_count * feat_count * pb_count
    lines, lanes = pieces[0][0].shape[1:]
    half = ex_count // pb_count
    chunk = (pb_count * ex_count, queries.shape[0] // half)
    vmem = pl.BlockSpec(memory_space=pltpu.VMEM)
    return pl.pallas_call(
        functools.partial(score_kernel, sizes, [piece[1:] for piece in pieces]),
        out_shape=[jax.ShapeDtypeStruct(chunk, jnp.float32)] * (half + 1)
        + [jax.ShapeDtypeStruct((ex_count, chunk[1]), jnp.float32)],
        in_specs=[vmem] * (3 + len(pieces)),
        out_specs=[vmem] * (half + 2),
        scratch_shapes=[
            pltpu.VMEM((examples, lines, lanes), jnp.float32),
            pltpu.VMEM((pb_count * lines, lanes), jnp.float32),
            pltpu.VMEM((half, *chunk), jnp.float32),
        ],
        compiler_params=pltpu.CompilerParams(vmem_limit_bytes=24 * 2**20),
        name="scores",
    )(queries, query_ids, example_ids, *[piece[0] for piece in pieces])


def gram_kernel(sizes, sources, kept_ref, *refs):
    ex_count, fp_count = sizes[0], sizes[1] * sizes[2]
    pieces = refs[: len(sources)]
    out_hbm, kept_out_ref, rows, left, right, result, sems = refs[len(sources) :]
    ex = lax.axis_index("ex")
    fp = lax.axis_index("feat") * sizes[2] + lax.axis_index("pb")
    examples, lines, lanes = rows.shape
    left_lines, right_lines = lines // ex_count, lines // fp_count
    kept_out_ref[...] = kept_ref[...]
    place_rows(sizes, sources, pieces, rows)
    block = rows[:, pl.ds(ex * left_lines, left_lines), :]
    left[...] = block.reshape(examples * left_lines, lanes)
    block = rows[:, pl.ds(fp * right_lines, right_lines), :]
    right[...] = block.reshape(examples * right_lines, lanes)
    across = jnp.concatenate(
        [right[pl.ds(j, examples, stride=right_lines), :] for j in range(right_lines)], axis=1
    ).astype(jnp.bfloat16)
    copies = []
    for i in range(left_lines):
        here = left[pl.ds(i, examples, stride=left_lines), :].T.astype(jnp.bfloat16)
        band = pl.ds(i * lanes, lanes)
        total = jnp.dot(here, across, preferred_element_type=jnp.float32)
        result[band, :] = total * (1.0 / examples)
        copies.append(
            pltpu.make_async_copy(result.at[band, :], out_hbm.at[band, :], sems.at[i])
        )
        copies[-1].start()
    for copy in copies:
        copy.wait()


def make_gram(sizes, pieces, kept):
    ex_count, fp_count = sizes[0], sizes[1] * sizes[2]
    examples = ex_count * fp_count
    lines, lanes = pieces[0][0].shape[1:]
    left_lines, right_lines = lines // ex_count, lines // fp_count
    shape = (left_lines * lanes, right_lines * lanes)
    return pl.pallas_call(
        functools.partial(gram_kernel, sizes, [piece[1:] for piece in pieces]),
        out_shape=[
            jax.ShapeDtypeStruct(shape, jnp.float32),
            jax.ShapeDtypeStruct(kept.shape, kept.dtype),
        ],
        in_specs=[pl.BlockSpec(memory_space=pltpu.VMEM)] * (1 + len(pieces)),
        out_specs=[pl.BlockSpec(memory_space=pl.ANY), pl.BlockSpec(memory_space=pltpu.VMEM)],
        scratch_shapes=[
            pltpu.VMEM((examples, lines, lanes), jnp.float32),
            pltpu.VMEM((examples * left_lines, lanes), jnp.float32),
            pltpu.VMEM((examples * right_lines, lanes), jnp.float32),
            pltpu.VMEM(shape, jnp.float32),
            pltpu.SemaphoreType.DMA((left_lines,)),
        ],
        compiler_params=pltpu.CompilerParams(vmem_limit_bytes=24 * 2**20),
        cost_estimate=pl.CostEstimate(
            flops=2 * 256 * shape[0] * shape[1],
            bytes_accessed=4 * shape[0] * shape[1],
            transcendentals=0,
        ),
        name="gram",
    )(kept, *[piece[0] for piece in pieces])


def to_owners(chunks, ex_count):
    half = ex_count // 2
    arrived = []
    for i, chunk in enumerate(chunks):
        pairs = []
        for e in range(ex_count):
            near, far = e // half, 1 - e // half
            pairs.append((e * 2 + near, (e ^ (i + 1 if i < half - 1 else 1)) * 2 + near))
            pairs.append((e * 2 + far, (e ^ (half + i)) * 2 + near))
        arrived.append(lax.ppermute(chunk, ("ex", "pb"), pairs))
    return sum(arrived)


def shards(
    activations, out_grads, act_proj, grad_proj, tok_counts, example_ids, query_sketch, query_ids
):
    ex_count, feat_count, pb_count = (lax.axis_size(axis) for axis in ("ex", "feat", "pb"))
    sizes = (ex_count, feat_count, pb_count)
    sketch = make_sketch(
        activations[0, 0], out_grads[0, 0], act_proj, grad_proj, tok_counts[0, 0]
    )
    pieces = gather_rows(sketch)
    width = query_ids.shape[0] // ex_count
    query_here = lax.dynamic_slice_in_dim(query_ids, lax.axis_index("ex") * width, width, 0)
    *chunks, own, is_open = partial_scores(
        sizes, query_sketch, query_here[None], example_ids, pieces
    )
    part = to_owners(chunks, ex_count)
    gram, own = make_gram(sizes, pieces, own)
    part = (part + own).reshape(pb_count, ex_count, -1)
    pb = lax.axis_index("pb")
    theirs = lax.dynamic_index_in_dim(part, 1 - pb, 0, keepdims=False)
    total = lax.dynamic_index_in_dim(part, pb, 0, keepdims=False) + exchange(theirs, "pb", 1)
    scores = jnp.where(is_open == 0.0, jnp.float32(0.0), total)
    return gram, scores.T[:, :, None]


def solution(mesh):
    return jax.shard_map(
        shards,
        mesh=mesh,
        in_specs=(
            P(("groups", "ex"), ("feat", "pb"), None, None),
            P(("groups", "ex"), ("feat", "pb"), None, None),
            P(),
            P(),
            P(("groups", "ex"), ("feat", "pb")),
            P("groups", ("feat", "pb")),
            P(("groups", "pb"), "ex"),
            P("groups"),
        ),
        out_specs=(P(("groups", "ex"), ("feat", "pb")), P(("groups", "ex"), None, ("feat", "pb"))),
        check_vma=False,
    )
```

```python
import functools
import math

import jax
import jax.numpy as jnp
from jax import lax
from jax.experimental import pallas as pl
from jax.experimental.pallas import tpu as pltpu
from jax.sharding import PartitionSpec as P

DAMPING = 0.1
NT = (((1,), (1,)), ((), ()))


def exchange(block, axis, step):
    return lax.ppermute(block, axis, [(i, i ^ step) for i in range(lax.axis_size(axis))])


def project_kernel(acts_hbm, grads_hbm, act_proj_hbm, grad_proj_hbm, act_low_ref, grad_low_ref, acts, grads, act_proj, grad_proj, sems):
    sources = (act_proj_hbm, acts_hbm, grad_proj_hbm, grads_hbm)
    targets = (act_proj, acts, grad_proj, grads)
    copies = [
        pltpu.make_async_copy(s, t, sems.at[i]) for i, (s, t) in enumerate(zip(sources, targets))
    ]
    for copy in copies:
        copy.start()
    for copy in copies[:2]:
        copy.wait()
    act_sum = lax.dot_general(acts[...], act_proj[...], NT, preferred_element_type=jnp.float32)
    for copy in copies[2:]:
        copy.wait()
    grad_sum = lax.dot_general(grad_proj[...], grads[...], NT, preferred_element_type=jnp.float32)
    act_low_ref[...] = act_sum.astype(jnp.bfloat16)
    grad_low_ref[...] = grad_sum.astype(jnp.bfloat16)


def make_sketch(acts, grads, act_proj, grad_proj, tok_count):
    seq_len, width = acts.shape
    hidden, rank = grad_proj.shape
    operands = (acts, grads, act_proj.T, grad_proj.T)
    act_low, grad_low = pl.pallas_call(
        project_kernel,
        out_shape=[
            jax.ShapeDtypeStruct((seq_len, rank), jnp.bfloat16),
            jax.ShapeDtypeStruct((rank, seq_len), jnp.bfloat16),
        ],
        in_specs=[pl.BlockSpec(memory_space=pl.ANY)] * 4,
        out_specs=[pl.BlockSpec(memory_space=pltpu.VMEM)] * 2,
        scratch_shapes=[pltpu.VMEM(x.shape, x.dtype) for x in operands]
        + [pltpu.SemaphoreType.DMA((4,))],
        compiler_params=pltpu.CompilerParams(vmem_limit_bytes=16 * 2**20),
        name="project",
    )(*[pltpu.with_memory_space_constraint(x, pltpu.HBM) for x in operands])
    mask = (jnp.arange(seq_len, dtype=jnp.int32) < tok_count).astype(jnp.bfloat16)
    outer = jnp.dot(grad_low * mask[None, :], act_low, preferred_element_type=jnp.float32)
    outer = outer * (1.0 / math.sqrt(seq_len))
    return outer.astype(jnp.bfloat16).reshape(rank // 2, 2 * rank)


def spread(block, distances):
    crossed = int(distances[0] == distances[1])
    pairs = [
        (e * len(distances) + p, (e ^ k) * len(distances) + (p ^ crossed))
        for e in range(lax.axis_size("ex"))
        for p, k in enumerate(distances)
    ]
    return lax.ppermute(block, ("ex", "pb"), pairs)


def gather_rows(sketch):
    ex_count = lax.axis_size("ex")
    fp_count = lax.axis_size(("feat", "pb"))
    own = sketch[None]
    block = jnp.concatenate([own] + [exchange(own, ("feat", "pb"), s) for s in range(1, fp_count)])
    pieces = [(block, (0, 0), 0)]
    for k in range(1, ex_count, 2):
        distances = (k, min(k + 1, ex_count - 1))
        near = spread(block, distances)
        pieces.append((near, distances, int(distances[0] == distances[1])))
        if distances[0] != distances[1]:
            pieces.append((exchange(near, "pb", 1), distances, 1))
    return pieces


def place_rows(sizes, sources, pieces, rows):
    ex_count, fp_count = sizes[0], sizes[1] * sizes[2]
    ex, pb = lax.axis_index("ex"), lax.axis_index("pb")
    fp = lax.axis_index("feat") * sizes[2] + pb
    for piece, (distances, core) in zip(pieces, sources):
        first, step = distances[core], distances[1 - core] - distances[core]
        where = ex ^ (first + step * pb)
        for s in range(fp_count):
            rows[(fp ^ core ^ s) * ex_count + where] = piece[s].astype(jnp.float32)


def score_kernel(sizes, sources, query_ref, query_ids_ref, example_ids_ref, *refs):
    ex_count, feat_count, pb_count = sizes
    half = ex_count // pb_count
    pieces, outs = refs[: len(sources)], refs[len(sources) : len(sources) + half]
    own_ref, open_ref, rows, scaled, chunks = refs[-5:]
    ex, feat = lax.axis_index("ex"), lax.axis_index("feat")
    near = lax.div(ex, half) == lax.axis_index("pb")
    here = lax.rem(ex, half)
    examples, lines, lanes = rows.shape
    block_lines = lines // ex_count
    mine = ex_count * pb_count
    place_rows(sizes, sources, pieces, rows)
    block = rows[:, pl.ds(ex * block_lines, block_lines), :]
    diag = jnp.sum(block * block, axis=0) / examples
    weight = 1.0 / (math.sqrt(lines * lanes) * (diag + DAMPING))
    own = rows[pl.ds(feat * mine, mine), pl.ds(ex * block_lines, block_lines), :]
    scaled[...] = (own * weight[None]).reshape(mine * block_lines, lanes)
    parts = [scaled[pl.ds(j, mine, stride=block_lines), :] for j in range(block_lines)]
    wide = jnp.concatenate(parts, axis=1)
    high = wide.astype(jnp.bfloat16)
    low = (wide - high.astype(jnp.float32)).astype(jnp.bfloat16)
    both = jnp.concatenate([high, low], axis=0)
    products = lax.dot_general(both, query_ref[...], NT, preferred_element_type=jnp.float32)
    result = products[:mine] + products[mine:]
    width = chunks.shape[2]
    for t in range(half):
        chunks[t] = result[:, t * width : (t + 1) * width]
    shift = near.astype(jnp.int32)
    for i in range(half - 1):
        outs[i][...] = chunks[here ^ (i + shift)]
    outs[half - 1][...] = jnp.where(near, 0.0, chunks[here ^ (half - 1)])
    own_ref[...] = jnp.where(near, chunks[here], 0.0)
    spans = chunks.shape[2] // query_ids_ref.shape[1]
    ids = [query_ids_ref[pl.ds(ex * spans + i, 1), :] for i in range(spans)]
    ids = jnp.concatenate(ids, axis=1)
    open_ref[...] = jnp.concatenate(
        [jnp.where(example_ids_ref[:, a : a + 1] == ids, 0.0, 1.0) for a in range(ex_count)]
    )


def partial_scores(sizes, queries, query_ids, example_ids, pieces):
    ex_count, feat_count, pb_count = sizes
    examples = ex_count * feat_count * pb_count
    lines, lanes = pieces[0][0].shape[1:]
    half = ex_count // pb_count
    chunk = (pb_count * ex_count, queries.shape[0] // half)
    vmem = pl.BlockSpec(memory_space=pltpu.VMEM)
    return pl.pallas_call(
        functools.partial(score_kernel, sizes, [piece[1:] for piece in pieces]),
        out_shape=[jax.ShapeDtypeStruct(chunk, jnp.float32)] * (half + 1)
        + [jax.ShapeDtypeStruct((ex_count, chunk[1]), jnp.float32)],
        in_specs=[vmem] * (3 + len(pieces)),
        out_specs=[vmem] * (half + 2),
        scratch_shapes=[
            pltpu.VMEM((examples, lines, lanes), jnp.float32),
            pltpu.VMEM((pb_count * lines, lanes), jnp.float32),
            pltpu.VMEM((half, *chunk), jnp.float32),
        ],
        compiler_params=pltpu.CompilerParams(vmem_limit_bytes=24 * 2**20),
        name="scores",
    )(queries, query_ids, example_ids, *[piece[0] for piece in pieces])


def gram_kernel(sizes, sources, kept_ref, *refs):
    ex_count, fp_count = sizes[0], sizes[1] * sizes[2]
    pieces = refs[: len(sources)]
    out_hbm, kept_out_ref, rows, left, right, result, sems = refs[len(sources) :]
    ex = lax.axis_index("ex")
    fp = lax.axis_index("feat") * sizes[2] + lax.axis_index("pb")
    examples, lines, lanes = rows.shape
    left_lines, right_lines = lines // ex_count, lines // fp_count
    kept_out_ref[...] = kept_ref[...]
    place_rows(sizes, sources, pieces, rows)
    block = rows[:, pl.ds(ex * left_lines, left_lines), :]
    left[...] = block.reshape(examples * left_lines, lanes)
    block = rows[:, pl.ds(fp * right_lines, right_lines), :]
    right[...] = block.reshape(examples * right_lines, lanes)
    across = jnp.concatenate(
        [right[pl.ds(j, examples, stride=right_lines), :] for j in range(right_lines)], axis=1
    ).astype(jnp.bfloat16)
    copies = []
    for i in range(left_lines):
        here = left[pl.ds(i, examples, stride=left_lines), :].T.astype(jnp.bfloat16)
        band = pl.ds(i * lanes, lanes)
        total = jnp.dot(here, across, preferred_element_type=jnp.float32)
        result[band, :] = total * (1.0 / examples)
        copies.append(
            pltpu.make_async_copy(result.at[band, :], out_hbm.at[band, :], sems.at[i])
        )
        copies[-1].start()
    for copy in copies:
        copy.wait()


def make_gram(sizes, pieces, kept):
    ex_count, fp_count = sizes[0], sizes[1] * sizes[2]
    examples = ex_count * fp_count
    lines, lanes = pieces[0][0].shape[1:]
    left_lines, right_lines = lines // ex_count, lines // fp_count
    shape = (left_lines * lanes, right_lines * lanes)
    return pl.pallas_call(
        functools.partial(gram_kernel, sizes, [piece[1:] for piece in pieces]),
        out_shape=[
            jax.ShapeDtypeStruct(shape, jnp.float32),
            jax.ShapeDtypeStruct(kept.shape, kept.dtype),
        ],
        in_specs=[pl.BlockSpec(memory_space=pltpu.VMEM)] * (1 + len(pieces)),
        out_specs=[pl.BlockSpec(memory_space=pl.ANY), pl.BlockSpec(memory_space=pltpu.VMEM)],
        scratch_shapes=[
            pltpu.VMEM((examples, lines, lanes), jnp.float32),
            pltpu.VMEM((examples * left_lines, lanes), jnp.float32),
            pltpu.VMEM((examples * right_lines, lanes), jnp.float32),
            pltpu.VMEM(shape, jnp.float32),
            pltpu.SemaphoreType.DMA((left_lines,)),
        ],
        compiler_params=pltpu.CompilerParams(vmem_limit_bytes=24 * 2**20),
        cost_estimate=pl.CostEstimate(
            flops=2 * 256 * shape[0] * shape[1],
            bytes_accessed=4 * shape[0] * shape[1],
            transcendentals=0,
        ),
        name="gram",
    )(kept, *[piece[0] for piece in pieces])


def to_owners(chunks, ex_count):
    half = ex_count // 2
    arrived = []
    for i, chunk in enumerate(chunks):
        pairs = []
        for e in range(ex_count):
            near, far = e // half, 1 - e // half
            pairs.append((e * 2 + near, (e ^ (i + 1 if i < half - 1 else 1)) * 2 + near))
            pairs.append((e * 2 + far, (e ^ (half + i)) * 2 + near))
        arrived.append(lax.ppermute(chunk, ("ex", "pb"), pairs))
    return sum(arrived)


def shards(
    activations, out_grads, act_proj, grad_proj, tok_counts, example_ids, query_sketch, query_ids
):
    ex_count, feat_count, pb_count = (lax.axis_size(axis) for axis in ("ex", "feat", "pb"))
    sizes = (ex_count, feat_count, pb_count)
    sketch = make_sketch(
        activations[0, 0], out_grads[0, 0], act_proj, grad_proj, tok_counts[0, 0]
    )
    pieces = gather_rows(sketch)
    width = query_ids.shape[0] // ex_count
    ids = query_ids.reshape(-1, min(width, 128))
    *chunks, own, is_open = partial_scores(sizes, query_sketch, ids, example_ids.T, pieces)
    part = to_owners(chunks, ex_count)
    gram, own = make_gram(sizes, pieces, own)
    part = (part + own).reshape(pb_count, ex_count, -1)
    pb = lax.axis_index("pb")
    theirs = lax.dynamic_index_in_dim(part, 1 - pb, 0, keepdims=False)
    total = lax.dynamic_index_in_dim(part, pb, 0, keepdims=False) + exchange(theirs, "pb", 1)
    scores = jnp.where(is_open == 0.0, jnp.float32(0.0), total)
    return gram, scores.T[:, :, None]


def solution(mesh):
    return jax.shard_map(
        shards,
        mesh=mesh,
        in_specs=(
            P(("groups", "ex"), ("feat", "pb"), None, None),
            P(("groups", "ex"), ("feat", "pb"), None, None),
            P(),
            P(),
            P(("groups", "ex"), ("feat", "pb")),
            P("groups", ("feat", "pb")),
            P(("groups", "pb"), "ex"),
            P("groups"),
        ),
        out_specs=(P(("groups", "ex"), ("feat", "pb")), P(("groups", "ex"), None, ("feat", "pb"))),
        check_vma=False,
    )
```

```python
import functools
import math

import jax
import jax.numpy as jnp
from jax import lax
from jax.experimental import pallas as pl
from jax.experimental.pallas import tpu as pltpu
from jax.sharding import PartitionSpec as P

DAMPING = 0.1
LANES = 128
NT = (((1,), (1,)), ((), ()))


def exchange(block, axis, step):
    return lax.ppermute(block, axis, [(i, i ^ step) for i in range(lax.axis_size(axis))])


def project_kernel(acts_hbm, grads_hbm, act_proj_hbm, grad_proj_hbm, act_low_ref, grad_low_ref, acts, grads, act_proj, grad_proj, sems):
    sources = (act_proj_hbm, acts_hbm, grad_proj_hbm, grads_hbm)
    targets = (act_proj, acts, grad_proj, grads)
    copies = [
        pltpu.make_async_copy(s, t, sems.at[i]) for i, (s, t) in enumerate(zip(sources, targets))
    ]
    for copy in copies:
        copy.start()
    for copy in copies[:2]:
        copy.wait()
    act_sum = lax.dot_general(acts[...], act_proj[...], NT, preferred_element_type=jnp.float32)
    for copy in copies[2:]:
        copy.wait()
    grad_sum = lax.dot_general(grad_proj[...], grads[...], NT, preferred_element_type=jnp.float32)
    act_low_ref[...] = act_sum.astype(jnp.bfloat16)
    grad_low_ref[...] = grad_sum.astype(jnp.bfloat16)


def make_sketch(acts, grads, act_proj, grad_proj, tok_count):
    seq_len, width = acts.shape
    hidden, rank = grad_proj.shape
    operands = (acts, grads, act_proj.T, grad_proj.T)
    act_low, grad_low = pl.pallas_call(
        project_kernel,
        out_shape=[
            jax.ShapeDtypeStruct((seq_len, rank), jnp.bfloat16),
            jax.ShapeDtypeStruct((rank, seq_len), jnp.bfloat16),
        ],
        in_specs=[pl.BlockSpec(memory_space=pl.ANY)] * 4,
        out_specs=[pl.BlockSpec(memory_space=pltpu.VMEM)] * 2,
        scratch_shapes=[pltpu.VMEM(x.shape, x.dtype) for x in operands]
        + [pltpu.SemaphoreType.DMA((4,))],
        compiler_params=pltpu.CompilerParams(vmem_limit_bytes=16 * 2**20),
        name="project",
    )(*[pltpu.with_memory_space_constraint(x, pltpu.HBM) for x in operands])
    mask = (jnp.arange(seq_len, dtype=jnp.int32) < tok_count).astype(jnp.bfloat16)
    outer = jnp.dot(grad_low * mask[None, :], act_low, preferred_element_type=jnp.float32)
    outer = outer * (1.0 / math.sqrt(seq_len))
    return outer.astype(jnp.bfloat16).reshape(rank * rank // LANES, LANES)


def spread(block, distances):
    crossed = int(distances[0] == distances[1])
    pairs = [
        (e * len(distances) + p, (e ^ k) * len(distances) + (p ^ crossed))
        for e in range(lax.axis_size("ex"))
        for p, k in enumerate(distances)
    ]
    return lax.ppermute(block, ("ex", "pb"), pairs)


def take(block, index):
    return lax.dynamic_index_in_dim(block, index, 1, keepdims=False)


def pairs_of_distances(ex_count):
    return [(k, min(k + 1, ex_count - 1)) for k in range(1, ex_count, 2)]


def gather_rows(sizes, sketch, queries):
    ex_count, feat_count, pb_count = sizes
    ex, feat, pb = (lax.axis_index(axis) for axis in ("ex", "feat", "pb"))
    fp_count, fp = feat_count * pb_count, feat * pb_count + pb
    ratio = ex_count // fp_count
    sketch, queries = lax.optimization_barrier((sketch, queries))
    own = sketch.reshape(1, ex_count, -1, LANES)
    others = exchange(queries, "pb", 1)
    block = jnp.concatenate([own] + [exchange(own, ("feat", "pb"), s) for s in range(1, fp_count)])
    by_fp = block.reshape(fp_count, fp_count, ratio, -1, LANES)

    def columns(index):
        return jnp.moveaxis(take(by_fp, index), 1, 0)

    pieces = [(block, (0, 0), 0)]
    for near, far in pairs_of_distances(ex_count):
        theirs = take(block, ex ^ (near + (far - near) * pb))[None]
        for_other = jnp.concatenate([theirs, columns(fp ^ 1)])
        if near == far:
            pieces.append((spread(for_other, (near, far)), (near, far), 1))
        else:
            both = spread(jnp.concatenate([columns(fp), for_other]), (near, far))
            pieces.append((both, (near, far), 0))
            pieces.append((exchange(both[ratio:], "pb", 1), (far, near), 1))
    return pieces, others


def place_rows(sizes, origins, pieces, left_rows, right_rows=None):
    ex_count, feat_count, pb_count = sizes
    ex, pb = lax.axis_index("ex"), lax.axis_index("pb")
    fp_count = feat_count * pb_count
    ratio = ex_count // fp_count
    fp = lax.axis_index("feat") * pb_count + pb
    for piece, (distances, other) in zip(pieces, origins):
        where = ex ^ (distances[0] + (distances[1] - distances[0]) * pb)
        whole = distances == (0, 0)
        left, right = (0, 1) if other else (ratio, 0)
        for s in range(fp_count):
            slot = (fp ^ other ^ s) * ex_count + where
            block = piece[s, ex] if whole else piece[left, s]
            left_rows[slot] = block.astype(jnp.float32)
            if right_rows is not None:
                block = piece[s, pl.ds(fp * ratio, ratio)] if whole else piece[right : right + ratio, s]
                right_rows[slot] = block.astype(jnp.float32).reshape(right_rows.shape[1:])


def score_kernel(
    sizes, origins, query_ref, other_query_ref, query_ids_ref, example_ids_ref, *refs
):
    ex_count, feat_count, pb_count = sizes
    pieces, refs = refs[: len(origins)], refs[len(origins) :]
    half = ex_count // pb_count
    outs = refs[:half]
    own_ref, open_ref, rows, scaled, chunks, products = refs[-6:]
    ex, feat = lax.axis_index("ex"), lax.axis_index("feat")
    near = lax.axis_index("pb") == 0
    here = lax.rem(ex, half)
    examples, block_lines, lanes = rows.shape
    mine = ex_count * pb_count
    place_rows(sizes, origins, pieces, rows)
    diag = jnp.sum(rows[...] * rows[...], axis=0) / examples
    weight = 1.0 / (math.sqrt(ex_count * block_lines * lanes) * (diag + DAMPING))
    own = rows[pl.ds(feat * mine, mine)]
    scaled[...] = (own * weight[None]).reshape(mine * block_lines, lanes)
    parts = [scaled[pl.ds(j, mine, stride=block_lines), :] for j in range(block_lines)]
    wide = jnp.concatenate(parts, axis=1)
    high = wide.astype(jnp.bfloat16)
    low = (wide - high.astype(jnp.float32)).astype(jnp.bfloat16)
    both = jnp.concatenate([high, low], axis=0)
    for side, queries in enumerate((query_ref, other_query_ref)):

        @pl.when(lax.div(ex, half) == side)
        def _():
            products[...] = lax.dot_general(
                both, queries[...], NT, preferred_element_type=jnp.float32
            )

    result = products[:mine, :] + products[mine:, :]
    width = chunks.shape[2]
    for t in range(half):
        chunks[t] = result[:, t * width : (t + 1) * width]
    shift = near.astype(jnp.int32)
    for i in range(half - 1):
        outs[i][...] = chunks[here ^ (i + shift)]
    outs[half - 1][...] = jnp.where(near, 0.0, chunks[here ^ (half - 1)])
    own_ref[...] = jnp.where(near, chunks[here], 0.0)
    spans = chunks.shape[2] // query_ids_ref.shape[1]
    ids = [query_ids_ref[pl.ds(ex * spans + i, 1), :] for i in range(spans)]
    ids = jnp.concatenate(ids, axis=1)
    open_ref[...] = jnp.concatenate(
        [jnp.where(example_ids_ref[:, a : a + 1] == ids, 0.0, 1.0) for a in range(ex_count)]
    )


def partial_scores(sizes, queries, other_queries, query_ids, example_ids, pieces):
    ex_count, feat_count, pb_count = sizes
    examples = ex_count * feat_count * pb_count
    lines, lanes = pieces[0][0].shape[2:]
    half = ex_count // pb_count
    chunk = (pb_count * ex_count, queries.shape[0] // half)
    vmem = pl.BlockSpec(memory_space=pltpu.VMEM)
    return pl.pallas_call(
        functools.partial(score_kernel, sizes, [piece[1:] for piece in pieces]),
        out_shape=[jax.ShapeDtypeStruct(chunk, jnp.float32)] * (half + 1)
        + [jax.ShapeDtypeStruct((ex_count, chunk[1]), jnp.float32)],
        in_specs=[vmem] * (4 + len(pieces)),
        out_specs=[vmem] * (half + 2),
        scratch_shapes=[
            pltpu.VMEM((examples, lines, lanes), jnp.float32),
            pltpu.VMEM((pb_count * ex_count * lines, lanes), jnp.float32),
            pltpu.VMEM((half, *chunk), jnp.float32),
            pltpu.VMEM((2 * chunk[0], queries.shape[0]), jnp.float32),
        ],
        compiler_params=pltpu.CompilerParams(vmem_limit_bytes=24 * 2**20),
        name="scores",
    )(queries, other_queries, query_ids, example_ids, *[piece[0] for piece in pieces])


def gram_kernel(sizes, origins, kept_ref, *refs):
    pieces, refs = refs[: len(origins)], refs[len(origins) :]
    out_hbm, kept_out_ref, left_rows, right_rows, left, right, result, sems = refs
    kept_out_ref[...] = kept_ref[...]
    examples, left_lines, lanes = left_rows.shape
    right_lines = right_rows.shape[1]
    place_rows(sizes, origins, pieces, left_rows, right_rows)
    left[...] = left_rows[...].reshape(examples * left_lines, lanes)
    right[...] = right_rows[...].reshape(examples * right_lines, lanes)
    across = jnp.concatenate(
        [right[pl.ds(j, examples, stride=right_lines), :] for j in range(right_lines)], axis=1
    ).astype(jnp.bfloat16)
    copies = []
    for i in range(left_lines):
        here = left[pl.ds(i, examples, stride=left_lines), :].T.astype(jnp.bfloat16)
        band = pl.ds(i * lanes, lanes)
        total = jnp.dot(here, across, preferred_element_type=jnp.float32)
        result[band, :] = total * (1.0 / examples)
        copies.append(
            pltpu.make_async_copy(result.at[band, :], out_hbm.at[band, :], sems.at[i])
        )
        copies[-1].start()
    for copy in copies:
        copy.wait()


def make_gram(sizes, pieces, kept):
    examples = sizes[0] * sizes[1] * sizes[2]
    left_lines = pieces[0][0].shape[2]
    right_lines = left_lines * sizes[0] // (sizes[1] * sizes[2])
    shape = (left_lines * LANES, right_lines * LANES)
    return pl.pallas_call(
        functools.partial(gram_kernel, sizes, [piece[1:] for piece in pieces]),
        out_shape=[
            jax.ShapeDtypeStruct(shape, jnp.float32),
            jax.ShapeDtypeStruct(kept.shape, kept.dtype),
        ],
        in_specs=[pl.BlockSpec(memory_space=pltpu.VMEM)] * (1 + len(pieces)),
        out_specs=[pl.BlockSpec(memory_space=pl.ANY), pl.BlockSpec(memory_space=pltpu.VMEM)],
        scratch_shapes=[
            pltpu.VMEM((examples, left_lines, LANES), jnp.float32),
            pltpu.VMEM((examples, right_lines, LANES), jnp.float32),
            pltpu.VMEM((examples * left_lines, LANES), jnp.float32),
            pltpu.VMEM((examples * right_lines, LANES), jnp.float32),
            pltpu.VMEM(shape, jnp.float32),
            pltpu.SemaphoreType.DMA((left_lines,)),
        ],
        compiler_params=pltpu.CompilerParams(vmem_limit_bytes=24 * 2**20),
        cost_estimate=pl.CostEstimate(
            flops=2 * 256 * shape[0] * shape[1],
            bytes_accessed=4 * shape[0] * shape[1],
            transcendentals=0,
        ),
        name="gram",
    )(kept, *[piece[0] for piece in pieces])


def to_owners(chunks, ex_count):
    half = ex_count // 2
    arrived = []
    for i, chunk in enumerate(chunks):
        pairs = []
        for e in range(ex_count):
            pairs.append((e * 2, (e ^ (i + 1 if i < half - 1 else 1)) * 2))
            pairs.append((e * 2 + 1, (e ^ (half + i)) * 2 + 1))
        arrived.append(lax.ppermute(chunk, ("ex", "pb"), pairs))
    return sum(arrived)


def shards(
    activations, out_grads, act_proj, grad_proj, tok_counts, example_ids, query_sketch, query_ids
):
    ex_count, feat_count, pb_count = (lax.axis_size(axis) for axis in ("ex", "feat", "pb"))
    sizes = (ex_count, feat_count, pb_count)
    sketch = make_sketch(
        activations[0, 0], out_grads[0, 0], act_proj, grad_proj, tok_counts[0, 0]
    )
    pieces, others = gather_rows(sizes, sketch, query_sketch)
    width = query_ids.shape[0] // ex_count
    ids = query_ids.reshape(-1, min(width, 128))
    *chunks, own, is_open = partial_scores(
        sizes, query_sketch, others, ids, example_ids.T, pieces
    )
    part = to_owners(chunks, ex_count)
    gram, own = make_gram(sizes, pieces, own)
    part = (part + own).reshape(pb_count, ex_count, -1)
    pb = lax.axis_index("pb")
    theirs = lax.dynamic_index_in_dim(part, 1 - pb, 0, keepdims=False)
    total = lax.dynamic_index_in_dim(part, pb, 0, keepdims=False) + exchange(theirs, "pb", 1)
    scores = jnp.where(is_open == 0.0, jnp.float32(0.0), total)
    return gram, scores.T[:, :, None]


def solution(mesh):
    return jax.shard_map(
        shards,
        mesh=mesh,
        in_specs=(
            P(("groups", "ex"), ("feat", "pb"), None, None),
            P(("groups", "ex"), ("feat", "pb"), None, None),
            P(),
            P(),
            P(("groups", "ex"), ("feat", "pb")),
            P("groups", ("feat", "pb")),
            P(("groups", "pb"), "ex"),
            P("groups"),
        ),
        out_specs=(P(("groups", "ex"), ("feat", "pb")), P(("groups", "ex"), None, ("feat", "pb"))),
        check_vma=False,
    )
```

```python
import functools
import math

import jax
import jax.numpy as jnp
from jax import lax
from jax.experimental import pallas as pl
from jax.experimental.pallas import tpu as pltpu
from jax.sharding import PartitionSpec as P

DAMPING = 0.1
LANES = 128
NT = (((1,), (1,)), ((), ()))


def exchange(block, axis, step):
    return lax.ppermute(block, axis, [(i, i ^ step) for i in range(lax.axis_size(axis))])


def project_kernel(
    acts_hbm, grads_hbm, act_proj_hbm, grad_proj_hbm, act_low_ref, grad_low_ref,
    acts, grads, act_proj, grad_proj, sems,
):
    sources = (act_proj_hbm, acts_hbm, grad_proj_hbm, grads_hbm)
    targets = (act_proj, acts, grad_proj, grads)
    copies = [
        pltpu.make_async_copy(s, t, sems.at[i]) for i, (s, t) in enumerate(zip(sources, targets))
    ]
    for copy, priority in zip(copies, (0, 0, 1, 0)):
        copy.start(priority=priority)
    for copy in copies[:2]:
        copy.wait()
    act_sum = lax.dot_general(acts[...], act_proj[...], NT, preferred_element_type=jnp.float32)
    for copy in copies[2:]:
        copy.wait()
    grad_sum = lax.dot_general(grad_proj[...], grads[...], NT, preferred_element_type=jnp.float32)
    act_low_ref[...] = act_sum.astype(jnp.bfloat16)
    grad_low_ref[...] = grad_sum.astype(jnp.bfloat16)


def make_sketch(acts, grads, act_proj, grad_proj, tok_count):
    seq_len, rank = acts.shape[0], act_proj.shape[1]
    operands = (acts, grads, act_proj.T, grad_proj.T)
    act_low, grad_low = pl.pallas_call(
        project_kernel,
        out_shape=[
            jax.ShapeDtypeStruct((seq_len, rank), jnp.bfloat16),
            jax.ShapeDtypeStruct((rank, seq_len), jnp.bfloat16),
        ],
        in_specs=[pl.BlockSpec(memory_space=pl.ANY)] * 4,
        out_specs=[pl.BlockSpec(memory_space=pltpu.VMEM)] * 2,
        scratch_shapes=[pltpu.VMEM(x.shape, x.dtype) for x in operands]
        + [pltpu.SemaphoreType.DMA((4,))],
        compiler_params=pltpu.CompilerParams(vmem_limit_bytes=16 * 2**20),
        name="project",
    )(*[pltpu.with_memory_space_constraint(x, pltpu.HBM) for x in operands])
    mask = (jnp.arange(seq_len, dtype=jnp.int32) < tok_count).astype(jnp.bfloat16)
    outer = jnp.dot(grad_low * mask[None, :], act_low, preferred_element_type=jnp.float32)
    outer = outer * (1.0 / math.sqrt(seq_len))
    return outer.astype(jnp.bfloat16).reshape(rank * rank // LANES, LANES)


def spread(block, distances):
    crossed = int(distances[0] == distances[1])
    pairs = [
        (e * len(distances) + p, (e ^ k) * len(distances) + (p ^ crossed))
        for e in range(lax.axis_size("ex"))
        for p, k in enumerate(distances)
    ]
    return lax.ppermute(block, ("ex", "pb"), pairs)


def take(block, index):
    return lax.dynamic_index_in_dim(block, index, 1, keepdims=False)


def pairs_of_distances(ex_count):
    return [(k, min(k + 1, ex_count - 1)) for k in range(1, ex_count, 2)]


def gather_rows(sizes, sketch, queries):
    ex_count, feat_count, pb_count = sizes
    ex, feat, pb = (lax.axis_index(axis) for axis in ("ex", "feat", "pb"))
    fp_count, fp = feat_count * pb_count, feat * pb_count + pb
    ratio = ex_count // fp_count
    own = sketch.reshape(1, ex_count, -1, LANES)
    own = jnp.concatenate([own, exchange(own, "pb", 1)])
    own, queries = lax.optimization_barrier((own, queries))
    others = exchange(queries, "pb", 1)
    line = [own]
    for k in range(1, feat_count):
        line.append(exchange(own, ("feat", "pb"), k * pb_count + 1)[::-1])
    block = jnp.concatenate(line)
    by_fp = block.reshape(fp_count, fp_count, ratio, -1, LANES)

    def columns(index):
        return jnp.moveaxis(take(by_fp, index), 1, 0)

    pieces = [(block, (0, 0), 0)]
    for near, far in pairs_of_distances(ex_count):
        theirs = take(block, ex ^ (near + (far - near) * pb))[None]
        for_other = jnp.concatenate([theirs, columns(fp ^ 1)])
        if near == far:
            pieces.append((spread(for_other, (near, far)), (near, far), 1))
        else:
            both = spread(jnp.concatenate([columns(fp), for_other]), (near, far))
            pieces.append((both, (near, far), 0))
            pieces.append((exchange(both[ratio:], "pb", 1), (far, near), 1))
    return pieces, others


def place_rows(sizes, origins, pieces, left_rows, right_rows=None):
    ex_count, feat_count, pb_count = sizes
    ex, pb = lax.axis_index("ex"), lax.axis_index("pb")
    fp_count = feat_count * pb_count
    ratio = ex_count // fp_count
    fp = lax.axis_index("feat") * pb_count + pb
    for piece, (distances, other) in zip(pieces, origins):
        where = ex ^ (distances[0] + (distances[1] - distances[0]) * pb)
        whole = distances == (0, 0)
        left, right = (0, 1) if other else (ratio, 0)
        for s in range(fp_count):
            slot = (fp ^ other ^ s) * ex_count + where
            block = piece[s, ex] if whole else piece[left, s]
            left_rows[slot] = block.astype(jnp.float32)
            if right_rows is not None:
                block = piece[s, pl.ds(fp * ratio, ratio)] if whole else piece[right : right + ratio, s]
                right_rows[slot] = block.astype(jnp.float32).reshape(right_rows.shape[1:])


def score_kernel(
    sizes, origins, query_ref, other_query_ref, query_ids_ref, example_ids_ref, *refs
):
    ex_count, feat_count, pb_count = sizes
    pieces, refs = refs[: len(origins)], refs[len(origins) :]
    half = ex_count // pb_count
    outs = refs[:half]
    own_ref, open_ref, rows, scaled, chunks = refs[-5:]
    ex, feat = lax.axis_index("ex"), lax.axis_index("feat")
    near = lax.axis_index("pb") == 0
    here = lax.rem(ex, half)
    examples, block_lines, lanes = rows.shape
    mine = ex_count * pb_count
    width = chunks.shape[2]
    for side, queries in enumerate((query_ref, other_query_ref)):

        @pl.when(lax.div(ex, half) == side)
        def _():
            place_rows(sizes, origins, pieces, rows)
            diag = jnp.sum(rows[...] * rows[...], axis=0) / examples
            weight = 1.0 / (math.sqrt(ex_count * block_lines * lanes) * (diag + DAMPING))
            own = rows[pl.ds(feat * mine, mine)]
            scaled[pl.ds(0, mine * block_lines), :] = (own * weight[None]).reshape(
                mine * block_lines, lanes
            )
            parts = [scaled[pl.ds(j, mine, stride=block_lines), :] for j in range(block_lines)]
            wide = jnp.concatenate(parts, axis=1)
            high = wide.astype(jnp.bfloat16)
            low = (wide - high.astype(jnp.float32)).astype(jnp.bfloat16)
            both = jnp.concatenate([high, low], axis=0)
            products = lax.dot_general(
                both, queries[...], NT, preferred_element_type=jnp.float32
            )
            result = products[:mine] + products[mine:]
            for t in range(half):
                chunks[t] = result[:, t * width : (t + 1) * width]

    shift = near.astype(jnp.int32)
    for i in range(half - 1):
        outs[i][...] = chunks[here ^ (i + shift)]
    outs[half - 1][...] = jnp.where(near, 0.0, chunks[here ^ (half - 1)])
    own_ref[...] = jnp.where(near, chunks[here], 0.0)
    spans = chunks.shape[2] // query_ids_ref.shape[1]
    ids = [query_ids_ref[pl.ds(ex * spans + i, 1), :] for i in range(spans)]
    ids = jnp.concatenate(ids, axis=1)
    for a in range(ex_count):
        open_ref[a] = jnp.where(example_ids_ref[:, a : a + 1] == ids, 0.0, 1.0)


def partial_scores(sizes, queries, other_queries, query_ids, example_ids, pieces):
    ex_count, feat_count, pb_count = sizes
    examples = ex_count * feat_count * pb_count
    lines, lanes = pieces[0][0].shape[2:]
    half = ex_count // pb_count
    chunk = (pb_count * ex_count, queries.shape[0] // half)
    vmem = pl.BlockSpec(memory_space=pltpu.VMEM)
    return pl.pallas_call(
        functools.partial(score_kernel, sizes, [piece[1:] for piece in pieces]),
        out_shape=[jax.ShapeDtypeStruct(chunk, jnp.float32)] * (half + 1)
        + [jax.ShapeDtypeStruct((ex_count, 1, chunk[1]), jnp.float32)],
        in_specs=[vmem] * (4 + len(pieces)),
        out_specs=[vmem] * (half + 2),
        scratch_shapes=[
            pltpu.VMEM((examples, lines, lanes), jnp.float32),
            pltpu.VMEM(((pb_count * ex_count + 1) * lines, lanes), jnp.float32),
            pltpu.VMEM((half, *chunk), jnp.float32),
        ],
        compiler_params=pltpu.CompilerParams(vmem_limit_bytes=24 * 2**20),
        name="scores",
    )(queries, other_queries, query_ids, example_ids, *[piece[0] for piece in pieces])


def gram_kernel(sizes, origins, kept_ref, *refs):
    pieces, refs = refs[: len(origins)], refs[len(origins) :]
    out_hbm, kept_out_ref, left_rows, right_rows, left, right, result, sems = refs
    kept_out_ref[...] = kept_ref[...]
    examples, left_lines, lanes = left_rows.shape
    right_lines = right_rows.shape[1]
    place_rows(sizes, origins, pieces, left_rows, right_rows)
    for rows, flat in ((left_rows, left), (right_rows, right)):
        lines = examples * rows.shape[1]
        flat[pl.ds(0, lines), :] = rows[...].reshape(lines, lanes)
    across = jnp.concatenate(
        [right[pl.ds(j, examples, stride=right_lines), :] for j in range(right_lines)], axis=1
    ).astype(jnp.bfloat16)
    copies = []
    for i in range(left_lines):
        here = left[pl.ds(i, examples, stride=left_lines), :].T.astype(jnp.bfloat16)
        band = pl.ds(i * lanes, lanes)
        total = jnp.dot(here, across, preferred_element_type=jnp.float32)
        result[band, :] = total * (1.0 / examples)
        copies.append(
            pltpu.make_async_copy(result.at[band, :], out_hbm.at[band, :], sems.at[i])
        )
        copies[-1].start()
    for copy in copies:
        copy.wait()


def make_gram(sizes, pieces, kept):
    examples = sizes[0] * sizes[1] * sizes[2]
    left_lines = pieces[0][0].shape[2]
    right_lines = left_lines * sizes[0] // (sizes[1] * sizes[2])
    shape = (left_lines * LANES, right_lines * LANES)
    return pl.pallas_call(
        functools.partial(gram_kernel, sizes, [piece[1:] for piece in pieces]),
        out_shape=[
            jax.ShapeDtypeStruct(shape, jnp.float32),
            jax.ShapeDtypeStruct(kept.shape, kept.dtype),
        ],
        in_specs=[pl.BlockSpec(memory_space=pltpu.VMEM)] * (1 + len(pieces)),
        out_specs=[pl.BlockSpec(memory_space=pl.ANY), pl.BlockSpec(memory_space=pltpu.VMEM)],
        scratch_shapes=[
            pltpu.VMEM((examples, left_lines, LANES), jnp.float32),
            pltpu.VMEM((examples, right_lines, LANES), jnp.float32),
            pltpu.VMEM(((examples + 1) * left_lines, LANES), jnp.float32),
            pltpu.VMEM(((examples + 1) * right_lines, LANES), jnp.float32),
            pltpu.VMEM(shape, jnp.float32),
            pltpu.SemaphoreType.DMA((left_lines,)),
        ],
        compiler_params=pltpu.CompilerParams(vmem_limit_bytes=24 * 2**20),
        cost_estimate=pl.CostEstimate(
            flops=2 * 256 * shape[0] * shape[1],
            bytes_accessed=4 * shape[0] * shape[1],
            transcendentals=0,
        ),
        name="gram",
    )(kept, *[piece[0] for piece in pieces])


def to_owners(chunks, ex_count):
    half = ex_count // 2
    arrived = []
    for i, chunk in enumerate(chunks):
        pairs = []
        for e in range(ex_count):
            pairs.append((e * 2, (e ^ (i + 1 if i < half - 1 else 1)) * 2))
            pairs.append((e * 2 + 1, (e ^ (half + i)) * 2 + 1))
        arrived.append(lax.ppermute(chunk, ("ex", "pb"), pairs))
    return sum(arrived)


def shards(
    activations, out_grads, act_proj, grad_proj, tok_counts, example_ids, query_sketch, query_ids
):
    ex_count, feat_count, pb_count = (lax.axis_size(axis) for axis in ("ex", "feat", "pb"))
    sizes = (ex_count, feat_count, pb_count)
    sketch = make_sketch(
        activations[0, 0], out_grads[0, 0], act_proj, grad_proj, tok_counts[0, 0]
    )
    pieces, others = gather_rows(sizes, sketch, query_sketch)
    width = query_ids.shape[0] // ex_count
    ids = query_ids.reshape(-1, min(width, 128))
    *chunks, own, is_open = partial_scores(
        sizes, query_sketch, others, ids, example_ids.T, pieces
    )
    part = to_owners(chunks, ex_count)
    gram, own = make_gram(sizes, pieces, own)
    part = (part + own).reshape(pb_count, ex_count, 1, -1)
    pb = lax.axis_index("pb")
    theirs = lax.dynamic_index_in_dim(part, 1 - pb, 0, keepdims=False)
    total = lax.dynamic_index_in_dim(part, pb, 0, keepdims=False) + exchange(theirs, "pb", 1)
    scores = jnp.where(is_open == 0.0, jnp.float32(0.0), total)
    return gram, scores.transpose(2, 0, 1)


def solution(mesh):
    return jax.shard_map(
        shards,
        mesh=mesh,
        in_specs=(
            P(("groups", "ex"), ("feat", "pb"), None, None),
            P(("groups", "ex"), ("feat", "pb"), None, None),
            P(),
            P(),
            P(("groups", "ex"), ("feat", "pb")),
            P("groups", ("feat", "pb")),
            P(("groups", "pb"), "ex"),
            P("groups"),
        ),
        out_specs=(P(("groups", "ex"), ("feat", "pb")), P(("groups", "ex"), None, ("feat", "pb"))),
        check_vma=False,
    )
```

```python
import functools
import math

import jax
import jax.numpy as jnp
from jax import lax
from jax.experimental import pallas as pl
from jax.experimental.pallas import tpu as pltpu
from jax.sharding import PartitionSpec as P

DAMPING = 0.1
LANES = 128
NT = (((1,), (1,)), ((), ()))


def exchange(block, axis, step):
    return lax.ppermute(block, axis, [(i, i ^ step) for i in range(lax.axis_size(axis))])


def project_kernel(
    acts_hbm, grads_hbm, act_proj_hbm, grad_proj_hbm, act_low_ref, grad_low_ref,
    acts, grads, act_proj, grad_proj, sems,
):
    sources = (act_proj_hbm, acts_hbm, grad_proj_hbm, grads_hbm)
    targets = (act_proj, acts, grad_proj, grads)
    copies = [
        pltpu.make_async_copy(s, t, sems.at[i]) for i, (s, t) in enumerate(zip(sources, targets))
    ]
    for copy, priority in zip(copies, (0, 0, 1, 0)):
        copy.start(priority=priority)
    for copy in copies[:2]:
        copy.wait()
    act_sum = lax.dot_general(acts[...], act_proj[...], NT, preferred_element_type=jnp.float32)
    for copy in copies[2:]:
        copy.wait()
    grad_sum = lax.dot_general(grad_proj[...], grads[...], NT, preferred_element_type=jnp.float32)
    act_low_ref[...] = act_sum.astype(jnp.bfloat16)
    grad_low_ref[...] = grad_sum.astype(jnp.bfloat16)


def make_sketch(acts, grads, act_proj, grad_proj, tok_count):
    seq_len, rank = acts.shape[0], act_proj.shape[1]
    operands = (acts, grads, act_proj.T, grad_proj.T)
    act_low, grad_low = pl.pallas_call(
        project_kernel,
        out_shape=[
            jax.ShapeDtypeStruct((seq_len, rank), jnp.bfloat16),
            jax.ShapeDtypeStruct((rank, seq_len), jnp.bfloat16),
        ],
        in_specs=[pl.BlockSpec(memory_space=pl.ANY)] * 4,
        out_specs=[pl.BlockSpec(memory_space=pltpu.VMEM)] * 2,
        scratch_shapes=[pltpu.VMEM(x.shape, x.dtype) for x in operands]
        + [pltpu.SemaphoreType.DMA((4,))],
        compiler_params=pltpu.CompilerParams(vmem_limit_bytes=16 * 2**20),
        name="project",
    )(*[pltpu.with_memory_space_constraint(x, pltpu.HBM) for x in operands])
    mask = (jnp.arange(seq_len, dtype=jnp.int32) < tok_count).astype(jnp.bfloat16)
    outer = jnp.dot(grad_low * mask[None, :], act_low, preferred_element_type=jnp.float32)
    outer = outer * (1.0 / math.sqrt(seq_len))
    return outer.astype(jnp.bfloat16).reshape(rank * rank // LANES, LANES)


def spread(block, distances):
    pairs = [
        (e * len(distances) + p, (e ^ k) * len(distances) + p)
        for e in range(lax.axis_size("ex"))
        for p, k in enumerate(distances)
    ]
    return lax.ppermute(block, ("ex", "pb"), pairs)


def take(block, index):
    return lax.dynamic_index_in_dim(block, index, 1, keepdims=False)


def pairs_of_distances(ex_count):
    return [(k, min(k + 1, ex_count - 1)) for k in range(1, ex_count, 2)]


def gather_rows(sizes, sketch, queries):
    ex_count, feat_count, pb_count = sizes
    ex, feat, pb = (lax.axis_index(axis) for axis in ("ex", "feat", "pb"))
    fp_count, fp = feat_count * pb_count, feat * pb_count + pb
    ratio = ex_count // fp_count
    own = sketch.reshape(1, ex_count, -1, LANES)
    own = jnp.concatenate([own, exchange(own, "pb", 1)])
    own, queries = lax.optimization_barrier((own, queries))
    others = exchange(queries, "pb", 1)
    line = [own]
    for k in range(1, feat_count):
        line.append(exchange(own, ("feat", "pb"), k * pb_count + 1)[::-1])
    block = jnp.concatenate(line)
    by_fp = block.reshape(fp_count, fp_count, ratio, -1, LANES)

    def columns(index):
        return jnp.moveaxis(take(by_fp, index), 1, 0)

    pieces = [(block, (0, 0), 0, None)]
    for near, far in pairs_of_distances(ex_count):
        theirs = take(block, ex ^ (near + (far - near) * pb))[None]
        if near == far:
            rows = spread(jnp.concatenate([theirs, columns(fp)]), (near, far))
            pieces.append((rows, (near, far), 0, 0))
        else:
            rows = jnp.concatenate([columns(fp), theirs, columns(fp ^ 1)])
            rows = spread(rows, (near, far))
            pieces.append((rows, (near, far), 0, ratio))
            pieces.append((exchange(rows[ratio:], "pb", 1), (far, near), 1, 0))
    return pieces, others


def place_rows(sizes, origins, pieces, left_rows, right_rows=None):
    ex_count, feat_count, pb_count = sizes
    ex, pb = lax.axis_index("ex"), lax.axis_index("pb")
    fp_count = feat_count * pb_count
    ratio = ex_count // fp_count
    fp = lax.axis_index("feat") * pb_count + pb
    for piece, (distances, other, left) in zip(pieces, origins):
        where = ex ^ (distances[0] + (distances[1] - distances[0]) * pb)
        for s in range(fp_count):
            slot = (fp ^ other ^ s) * ex_count + where
            block = piece[s, ex] if left is None else piece[left, s]
            left_rows[slot] = block.astype(jnp.float32)
            if right_rows is not None:
                if left is None:
                    block = piece[s, pl.ds(fp * ratio, ratio)]
                else:
                    right = 0 if left else 1
                    block = piece[right : right + ratio, s]
                right_rows[slot] = block.astype(jnp.float32).reshape(right_rows.shape[1:])


def score_kernel(
    sizes, origins, query_ref, other_query_ref, query_ids_ref, example_ids_ref, *refs
):
    ex_count, feat_count, pb_count = sizes
    pieces, refs = refs[: len(origins)], refs[len(origins) :]
    half = ex_count // pb_count
    outs = refs[:half]
    own_ref, open_ref, rows, scaled, chunks = refs[-5:]
    ex, feat = lax.axis_index("ex"), lax.axis_index("feat")
    near = lax.axis_index("pb") == 0
    here = lax.rem(ex, half)
    examples, block_lines, lanes = rows.shape
    mine = ex_count * pb_count
    width = chunks.shape[2]
    for side, queries in enumerate((query_ref, other_query_ref)):

        @pl.when(lax.div(ex, half) == side)
        def _():
            place_rows(sizes, origins, pieces, rows)
            diag = jnp.sum(rows[...] * rows[...], axis=0) / examples
            weight = 1.0 / (math.sqrt(ex_count * block_lines * lanes) * (diag + DAMPING))
            own = rows[pl.ds(feat * mine, mine)]
            scaled[pl.ds(0, mine * block_lines), :] = (own * weight[None]).reshape(
                mine * block_lines, lanes
            )
            parts = [scaled[pl.ds(j, mine, stride=block_lines), :] for j in range(block_lines)]
            wide = jnp.concatenate(parts, axis=1)
            high = wide.astype(jnp.bfloat16)
            low = (wide - high.astype(jnp.float32)).astype(jnp.bfloat16)
            both = jnp.concatenate([high, low], axis=0)
            products = lax.dot_general(
                both, queries[...], NT, preferred_element_type=jnp.float32
            )
            result = products[:mine] + products[mine:]
            for t in range(half):
                chunks[t] = result[:, t * width : (t + 1) * width]

    shift = near.astype(jnp.int32)
    for i in range(half - 1):
        outs[i][...] = chunks[here ^ (i + shift)]
    outs[half - 1][...] = jnp.where(near, 0.0, chunks[here ^ (half - 1)])
    own_ref[...] = jnp.where(near, chunks[here], 0.0)
    spans = chunks.shape[2] // query_ids_ref.shape[1]
    ids = [query_ids_ref[pl.ds(ex * spans + i, 1), :] for i in range(spans)]
    ids = jnp.concatenate(ids, axis=1)
    for a in range(ex_count):
        open_ref[a] = jnp.where(example_ids_ref[:, a : a + 1] == ids, 0.0, 1.0)


def partial_scores(sizes, queries, other_queries, query_ids, example_ids, pieces):
    ex_count, feat_count, pb_count = sizes
    examples = ex_count * feat_count * pb_count
    lines, lanes = pieces[0][0].shape[2:]
    half = ex_count // pb_count
    chunk = (pb_count * ex_count, queries.shape[0] // half)
    vmem = pl.BlockSpec(memory_space=pltpu.VMEM)
    return pl.pallas_call(
        functools.partial(score_kernel, sizes, [piece[1:] for piece in pieces]),
        out_shape=[jax.ShapeDtypeStruct(chunk, jnp.float32)] * (half + 1)
        + [jax.ShapeDtypeStruct((ex_count, 1, chunk[1]), jnp.float32)],
        in_specs=[vmem] * (4 + len(pieces)),
        out_specs=[vmem] * (half + 2),
        scratch_shapes=[
            pltpu.VMEM((examples, lines, lanes), jnp.float32),
            pltpu.VMEM(((pb_count * ex_count + 1) * lines, lanes), jnp.float32),
            pltpu.VMEM((half, *chunk), jnp.float32),
        ],
        compiler_params=pltpu.CompilerParams(vmem_limit_bytes=24 * 2**20),
        name="scores",
    )(queries, other_queries, query_ids, example_ids, *[piece[0] for piece in pieces])


def gram_kernel(sizes, origins, kept_ref, *refs):
    pieces, refs = refs[: len(origins)], refs[len(origins) :]
    out_hbm, kept_out_ref, left_rows, right_rows, left, right, result, sems = refs
    kept_out_ref[...] = kept_ref[...]
    examples, left_lines, lanes = left_rows.shape
    right_lines = right_rows.shape[1]
    place_rows(sizes, origins, pieces, left_rows, right_rows)
    for rows, flat in ((left_rows, left), (right_rows, right)):
        lines = examples * rows.shape[1]
        flat[pl.ds(0, lines), :] = rows[...].reshape(lines, lanes)
    across = jnp.concatenate(
        [right[pl.ds(j, examples, stride=right_lines), :] for j in range(right_lines)], axis=1
    ).astype(jnp.bfloat16)
    copies = []
    for i in range(left_lines):
        here = left[pl.ds(i, examples, stride=left_lines), :].T.astype(jnp.bfloat16)
        band = pl.ds(i * lanes, lanes)
        total = jnp.dot(here, across, preferred_element_type=jnp.float32)
        result[band, :] = total * (1.0 / examples)
        copies.append(
            pltpu.make_async_copy(result.at[band, :], out_hbm.at[band, :], sems.at[i])
        )
        copies[-1].start()
    for copy in copies:
        copy.wait()


def make_gram(sizes, pieces, kept):
    examples = sizes[0] * sizes[1] * sizes[2]
    left_lines = pieces[0][0].shape[2]
    right_lines = left_lines * sizes[0] // (sizes[1] * sizes[2])
    shape = (left_lines * LANES, right_lines * LANES)
    return pl.pallas_call(
        functools.partial(gram_kernel, sizes, [piece[1:] for piece in pieces]),
        out_shape=[
            jax.ShapeDtypeStruct(shape, jnp.float32),
            jax.ShapeDtypeStruct(kept.shape, kept.dtype),
        ],
        in_specs=[pl.BlockSpec(memory_space=pltpu.VMEM)] * (1 + len(pieces)),
        out_specs=[pl.BlockSpec(memory_space=pl.ANY), pl.BlockSpec(memory_space=pltpu.VMEM)],
        scratch_shapes=[
            pltpu.VMEM((examples, left_lines, LANES), jnp.float32),
            pltpu.VMEM((examples, right_lines, LANES), jnp.float32),
            pltpu.VMEM(((examples + 1) * left_lines, LANES), jnp.float32),
            pltpu.VMEM(((examples + 1) * right_lines, LANES), jnp.float32),
            pltpu.VMEM(shape, jnp.float32),
            pltpu.SemaphoreType.DMA((left_lines,)),
        ],
        compiler_params=pltpu.CompilerParams(vmem_limit_bytes=24 * 2**20),
        cost_estimate=pl.CostEstimate(
            flops=2 * 256 * shape[0] * shape[1],
            bytes_accessed=4 * shape[0] * shape[1],
            transcendentals=0,
        ),
        name="gram",
    )(kept, *[piece[0] for piece in pieces])


def to_owners(chunks, sizes):
    ex_count, feat_count, pb_count = sizes
    half = ex_count // pb_count

    def device(e, f, p):
        return (e * feat_count + f) * pb_count + p

    arrived = []
    for i, chunk in enumerate(chunks):
        pairs = []
        for e in range(ex_count):
            for f in range(feat_count):
                near = device(e ^ (i + 1), f, 0) if i < half - 1 else device(e, f ^ 1, 0)
                pairs.append((device(e, f, 0), near))
                pairs.append((device(e, f, 1), device(e ^ (half + i), f, 1)))
        arrived.append(lax.ppermute(chunk, ("ex", "feat", "pb"), pairs))
    return sum(arrived)


def shards(
    activations, out_grads, act_proj, grad_proj, tok_counts, example_ids, query_sketch, query_ids
):
    ex_count, feat_count, pb_count = (lax.axis_size(axis) for axis in ("ex", "feat", "pb"))
    sizes = (ex_count, feat_count, pb_count)
    sketch = make_sketch(
        activations[0, 0], out_grads[0, 0], act_proj, grad_proj, tok_counts[0, 0]
    )
    pieces, others = gather_rows(sizes, sketch, query_sketch)
    width = query_ids.shape[0] // ex_count
    ids = query_ids.reshape(-1, min(width, 128))
    *chunks, own, is_open = partial_scores(
        sizes, query_sketch, others, ids, example_ids.T, pieces
    )
    part = to_owners(chunks, sizes)
    gram, own = make_gram(sizes, pieces, own)
    part = (part + own).reshape(pb_count, ex_count, 1, -1)
    pb = lax.axis_index("pb")
    theirs = lax.dynamic_index_in_dim(part, 1 - pb, 0, keepdims=False)
    total = lax.dynamic_index_in_dim(part, pb, 0, keepdims=False) + exchange(theirs, "pb", 1)
    scores = jnp.where(is_open == 0.0, jnp.float32(0.0), total)
    return gram, scores.transpose(2, 0, 1)


def solution(mesh):
    return jax.shard_map(
        shards,
        mesh=mesh,
        in_specs=(
            P(("groups", "ex"), ("feat", "pb"), None, None),
            P(("groups", "ex"), ("feat", "pb"), None, None),
            P(),
            P(),
            P(("groups", "ex"), ("feat", "pb")),
            P("groups", ("feat", "pb")),
            P(("groups", "pb"), "ex"),
            P("groups"),
        ),
        out_specs=(P(("groups", "ex"), ("feat", "pb")), P(("groups", "ex"), None, ("feat", "pb"))),
        check_vma=False,
    )
```

```python
import functools
import math

import jax
import jax.numpy as jnp
from jax import lax
from jax.experimental import pallas as pl
from jax.experimental.pallas import tpu as pltpu
from jax.sharding import PartitionSpec as P

DAMPING = 0.1
LANES = 128
NT = (((1,), (1,)), ((), ()))


def exchange(block, axis, step):
    return lax.ppermute(block, axis, [(i, i ^ step) for i in range(lax.axis_size(axis))])


def sketch_kernel(
    acts_hbm, grads_hbm, act_proj_hbm, grad_proj_hbm, keep_ref, out_ref,
    acts, grads, act_proj, grad_proj, turned, sems,
):
    sources = (act_proj_hbm, acts_hbm, grad_proj_hbm, grads_hbm)
    targets = (act_proj, acts, grad_proj, grads)
    copies = [
        pltpu.make_async_copy(s, t, sems.at[i]) for i, (s, t) in enumerate(zip(sources, targets))
    ]
    for copy, priority in zip(copies, (0, 0, 1, 0)):
        copy.start(priority=priority)
    for copy in copies[:2]:
        copy.wait()
    act_sum = lax.dot_general(acts[...], act_proj[...], NT, preferred_element_type=jnp.float32)
    act_low = act_sum.astype(jnp.bfloat16)
    for copy in copies[2:]:
        copy.wait()
    grad_sum = lax.dot_general(grad_proj[...], grads[...], NT, preferred_element_type=jnp.float32)
    rank, seq_len = grad_sum.shape
    turned[pl.ds(0, rank), :] = grad_sum * keep_ref[...]
    halves = [
        jnp.dot(
            turned[pl.ds(side, rank // 2, stride=2), :].astype(jnp.bfloat16),
            act_low,
            preferred_element_type=jnp.float32,
        )
        for side in range(2)
    ]
    outer = jnp.concatenate(halves, axis=1) * (1.0 / math.sqrt(seq_len))
    out_ref[...] = outer.astype(jnp.bfloat16)


def make_sketch(acts, grads, act_proj, grad_proj, tok_count):
    seq_len, rank = acts.shape[0], act_proj.shape[1]
    operands = (acts, grads, act_proj.T, grad_proj.T)
    keep = (jnp.arange(seq_len, dtype=jnp.int32) < tok_count).astype(jnp.float32)
    vmem = pl.BlockSpec(memory_space=pltpu.VMEM)
    return pl.pallas_call(
        sketch_kernel,
        out_shape=jax.ShapeDtypeStruct((rank // 2, 2 * rank), jnp.bfloat16),
        in_specs=[pl.BlockSpec(memory_space=pl.ANY)] * 4 + [vmem],
        out_specs=vmem,
        scratch_shapes=[pltpu.VMEM(x.shape, x.dtype) for x in operands]
        + [pltpu.VMEM((rank + 8, seq_len), jnp.float32), pltpu.SemaphoreType.DMA((4,))],
        compiler_params=pltpu.CompilerParams(vmem_limit_bytes=16 * 2**20),
        name="sketch",
    )(*[pltpu.with_memory_space_constraint(x, pltpu.HBM) for x in operands], keep[None])


def spread(block, distances):
    pairs = [
        (e * len(distances) + p, (e ^ k) * len(distances) + p)
        for e in range(lax.axis_size("ex"))
        for p, k in enumerate(distances)
    ]
    return lax.ppermute(block, ("ex", "pb"), pairs)


def take(block, index):
    return lax.dynamic_index_in_dim(block, index, 1, keepdims=False)


def pairs_of_distances(ex_count):
    return [(k, min(k + 1, ex_count - 1)) for k in range(1, ex_count, 2)]


def gather_rows(sizes, sketch, queries):
    ex_count, feat_count, pb_count = sizes
    ex, feat, pb = (lax.axis_index(axis) for axis in ("ex", "feat", "pb"))
    fp_count, fp = feat_count * pb_count, feat * pb_count + pb
    ratio = ex_count // fp_count
    others = exchange(queries, "pb", 1)
    own = sketch.reshape(1, ex_count, -1, LANES)
    own = jnp.concatenate([own, exchange(own, "pb", 1)])
    line = [own]
    for k in range(1, feat_count):
        line.append(exchange(own, ("feat", "pb"), k * pb_count + 1)[::-1])
    block = jnp.concatenate(line)
    by_fp = block.reshape(fp_count, fp_count, ratio, -1, LANES)

    def columns(index):
        return jnp.moveaxis(take(by_fp, index), 1, 0)

    pieces = [(block, (0, 0), 0, None)]
    for near, far in pairs_of_distances(ex_count):
        theirs = take(block, ex ^ (near + (far - near) * pb))[None]
        if near == far:
            rows = spread(jnp.concatenate([theirs, columns(fp)]), (near, far))
            pieces.append((rows, (near, far), 0, 0))
        else:
            rows = jnp.concatenate([columns(fp), theirs, columns(fp ^ 1)])
            rows = spread(rows, (near, far))
            pieces.append((rows, (near, far), 0, ratio))
            pieces.append((exchange(rows[ratio:], "pb", 1), (far, near), 1, 0))
    return pieces, others


def place_rows(sizes, origins, pieces, left_rows, right_rows=None):
    ex_count, feat_count, pb_count = sizes
    ex, pb = lax.axis_index("ex"), lax.axis_index("pb")
    fp_count = feat_count * pb_count
    ratio = ex_count // fp_count
    fp = lax.axis_index("feat") * pb_count + pb
    for piece, (distances, other, left) in zip(pieces, origins):
        where = ex ^ (distances[0] + (distances[1] - distances[0]) * pb)
        for s in range(fp_count):
            slot = (fp ^ other ^ s) * ex_count + where
            block = piece[s, ex] if left is None else piece[left, s]
            left_rows[slot] = block.astype(jnp.float32)
            if right_rows is not None:
                if left is None:
                    block = piece[s, pl.ds(fp * ratio, ratio)]
                else:
                    right = 0 if left else 1
                    block = piece[right : right + ratio, s]
                right_rows[slot] = block.astype(jnp.float32).reshape(right_rows.shape[1:])


def score_kernel(sizes, origins, query_ref, other_query_ref, *refs):
    ex_count, feat_count, pb_count = sizes
    pieces, refs = refs[: len(origins)], refs[len(origins) :]
    half = ex_count // pb_count
    outs = refs[:half]
    own_ref, rows, scaled, chunks = refs[-4:]
    ex, feat = lax.axis_index("ex"), lax.axis_index("feat")
    near = lax.axis_index("pb") == 0
    here = lax.rem(ex, half)
    examples, block_lines, lanes = rows.shape
    mine = ex_count * pb_count
    width = chunks.shape[2]
    for side, queries in enumerate((query_ref, other_query_ref)):

        @pl.when(lax.div(ex, half) == side)
        def _():
            place_rows(sizes, origins, pieces, rows)
            diag = jnp.sum(rows[...] * rows[...], axis=0) / examples
            weight = 1.0 / (math.sqrt(ex_count * block_lines * lanes) * (diag + DAMPING))
            own = rows[pl.ds(feat * mine, mine)]
            scaled[pl.ds(0, mine * block_lines), :] = (own * weight[None]).reshape(
                mine * block_lines, lanes
            )
            parts = [scaled[pl.ds(j, mine, stride=block_lines), :] for j in range(block_lines)]
            wide = jnp.concatenate(parts, axis=1)
            high = wide.astype(jnp.bfloat16)
            low = (wide - high.astype(jnp.float32)).astype(jnp.bfloat16)
            both = jnp.concatenate([high, low], axis=0)
            products = lax.dot_general(
                both, queries[...], NT, preferred_element_type=jnp.float32
            )
            result = products[:mine] + products[mine:]
            for t in range(half):
                chunks[t] = result[:, t * width : (t + 1) * width]

    shift = near.astype(jnp.int32)
    for i in range(half - 1):
        outs[i][...] = chunks[here ^ (i + shift)]
    outs[half - 1][...] = jnp.where(near, 0.0, chunks[here ^ (half - 1)])
    own_ref[...] = jnp.where(near, chunks[here], 0.0)


def partial_scores(sizes, queries, other_queries, pieces):
    ex_count, feat_count, pb_count = sizes
    examples = ex_count * feat_count * pb_count
    lines, lanes = pieces[0][0].shape[2:]
    half = ex_count // pb_count
    chunk = (pb_count * ex_count, queries.shape[0] // half)
    vmem = pl.BlockSpec(memory_space=pltpu.VMEM)
    return pl.pallas_call(
        functools.partial(score_kernel, sizes, [piece[1:] for piece in pieces]),
        out_shape=[jax.ShapeDtypeStruct(chunk, jnp.float32)] * (half + 1),
        in_specs=[vmem] * (2 + len(pieces)),
        out_specs=[vmem] * (half + 1),
        scratch_shapes=[
            pltpu.VMEM((examples, lines, lanes), jnp.float32),
            pltpu.VMEM(((pb_count * ex_count + 1) * lines, lanes), jnp.float32),
            pltpu.VMEM((half, *chunk), jnp.float32),
        ],
        compiler_params=pltpu.CompilerParams(vmem_limit_bytes=24 * 2**20),
        name="scores",
    )(queries, other_queries, *[piece[0] for piece in pieces])


def gram_kernel(sizes, origins, kept_ref, query_ids_ref, example_ids_ref, *refs):
    pieces, refs = refs[: len(origins)], refs[len(origins) :]
    out_hbm, kept_out_ref, open_ref, left_rows, right_rows, left, right, result, sems = refs
    kept_out_ref[...] = kept_ref[...]
    ex = lax.axis_index("ex")
    spans = open_ref.shape[2] // query_ids_ref.shape[1]
    ids = [query_ids_ref[pl.ds(ex * spans + i, 1), :] for i in range(spans)]
    ids = jnp.concatenate(ids, axis=1)
    for a in range(open_ref.shape[0]):
        open_ref[a] = jnp.where(example_ids_ref[:, a : a + 1] == ids, 0.0, 1.0)
    examples, left_lines, lanes = left_rows.shape
    right_lines = right_rows.shape[1]
    place_rows(sizes, origins, pieces, left_rows, right_rows)
    for rows, flat in ((left_rows, left), (right_rows, right)):
        lines = examples * rows.shape[1]
        flat[pl.ds(0, lines), :] = rows[...].reshape(lines, lanes)
    across = jnp.concatenate(
        [right[pl.ds(j, examples, stride=right_lines), :] for j in range(right_lines)], axis=1
    ).astype(jnp.bfloat16)
    copies = []
    for i in range(left_lines):
        here = left[pl.ds(i, examples, stride=left_lines), :].T.astype(jnp.bfloat16)
        band = pl.ds(i * lanes, lanes)
        total = jnp.dot(here, across, preferred_element_type=jnp.float32)
        result[band, :] = total * (1.0 / examples)
        copies.append(
            pltpu.make_async_copy(result.at[band, :], out_hbm.at[band, :], sems.at[i])
        )
        copies[-1].start()
    for copy in copies:
        copy.wait()


def make_gram(sizes, pieces, kept, query_ids, example_ids):
    examples = sizes[0] * sizes[1] * sizes[2]
    left_lines = pieces[0][0].shape[2]
    right_lines = left_lines * sizes[0] // (sizes[1] * sizes[2])
    shape = (left_lines * LANES, right_lines * LANES)
    vmem = pl.BlockSpec(memory_space=pltpu.VMEM)
    return pl.pallas_call(
        functools.partial(gram_kernel, sizes, [piece[1:] for piece in pieces]),
        out_shape=[
            jax.ShapeDtypeStruct(shape, jnp.float32),
            jax.ShapeDtypeStruct(kept.shape, kept.dtype),
            jax.ShapeDtypeStruct((sizes[0], 1, kept.shape[1]), jnp.float32),
        ],
        in_specs=[vmem] * (3 + len(pieces)),
        out_specs=[pl.BlockSpec(memory_space=pl.ANY), vmem, vmem],
        scratch_shapes=[
            pltpu.VMEM((examples, left_lines, LANES), jnp.float32),
            pltpu.VMEM((examples, right_lines, LANES), jnp.float32),
            pltpu.VMEM(((examples + 1) * left_lines, LANES), jnp.float32),
            pltpu.VMEM(((examples + 1) * right_lines, LANES), jnp.float32),
            pltpu.VMEM(shape, jnp.float32),
            pltpu.SemaphoreType.DMA((left_lines,)),
        ],
        compiler_params=pltpu.CompilerParams(vmem_limit_bytes=24 * 2**20),
        cost_estimate=pl.CostEstimate(
            flops=2 * 256 * shape[0] * shape[1],
            bytes_accessed=4 * shape[0] * shape[1],
            transcendentals=0,
        ),
        name="gram",
    )(kept, query_ids, example_ids, *[piece[0] for piece in pieces])


def to_owners(chunks, sizes):
    ex_count, feat_count, pb_count = sizes
    half = ex_count // pb_count

    def device(e, f, p):
        return (e * feat_count + f) * pb_count + p

    arrived = []
    for i, chunk in enumerate(chunks):
        pairs = []
        for e in range(ex_count):
            for f in range(feat_count):
                near = device(e ^ (i + 1), f, 0) if i < half - 1 else device(e, f ^ 1, 0)
                pairs.append((device(e, f, 0), near))
                pairs.append((device(e, f, 1), device(e ^ (half + i), f, 1)))
        arrived.append(lax.ppermute(chunk, ("ex", "feat", "pb"), pairs))
    return sum(arrived)


def shards(
    activations, out_grads, act_proj, grad_proj, tok_counts, example_ids, query_sketch, query_ids
):
    ex_count, feat_count, pb_count = (lax.axis_size(axis) for axis in ("ex", "feat", "pb"))
    sizes = (ex_count, feat_count, pb_count)
    sketch = make_sketch(
        activations[0, 0], out_grads[0, 0], act_proj, grad_proj, tok_counts[0, 0]
    )
    pieces, others = gather_rows(sizes, sketch, query_sketch)
    width = query_ids.shape[0] // ex_count
    ids = query_ids.reshape(-1, min(width, 128))
    *chunks, own = partial_scores(sizes, query_sketch, others, pieces)
    part = to_owners(chunks, sizes)
    gram, own, is_open = make_gram(sizes, pieces, own, ids, example_ids.T)
    part = (part + own).reshape(pb_count, ex_count, 1, -1)
    pb = lax.axis_index("pb")
    theirs = lax.dynamic_index_in_dim(part, 1 - pb, 0, keepdims=False)
    total = lax.dynamic_index_in_dim(part, pb, 0, keepdims=False) + exchange(theirs, "pb", 1)
    scores = jnp.where(is_open == 0.0, jnp.float32(0.0), total)
    return gram, scores.transpose(2, 0, 1)


def solution(mesh):
    return jax.shard_map(
        shards,
        mesh=mesh,
        in_specs=(
            P(("groups", "ex"), ("feat", "pb"), None, None),
            P(("groups", "ex"), ("feat", "pb"), None, None),
            P(),
            P(),
            P(("groups", "ex"), ("feat", "pb")),
            P("groups", ("feat", "pb")),
            P(("groups", "pb"), "ex"),
            P("groups"),
        ),
        out_specs=(P(("groups", "ex"), ("feat", "pb")), P(("groups", "ex"), None, ("feat", "pb"))),
        check_vma=False,
    )
```

```python
import functools
import math

import jax
import jax.numpy as jnp
from jax import lax
from jax.experimental import pallas as pl
from jax.experimental.pallas import tpu as pltpu
from jax.sharding import PartitionSpec as P

DAMPING = 0.1
LANES = 128
NT = (((1,), (1,)), ((), ()))


def exchange(block, axis, step):
    return lax.ppermute(block, axis, [(i, i ^ step) for i in range(lax.axis_size(axis))])


def sketch_kernel(
    acts_hbm, grads_hbm, act_proj_hbm, grad_proj_hbm, keep_ref, out_ref,
    acts, grads, act_proj, grad_proj, turned, sems,
):
    sources = (act_proj_hbm, acts_hbm, grad_proj_hbm, grads_hbm)
    targets = (act_proj, acts, grad_proj, grads)
    copies = [
        pltpu.make_async_copy(s, t, sems.at[i]) for i, (s, t) in enumerate(zip(sources, targets))
    ]
    for copy, priority in zip(copies, (0, 0, 1, 0)):
        copy.start(priority=priority)
    for copy in copies[:2]:
        copy.wait()
    act_sum = lax.dot_general(acts[...], act_proj[...], NT, preferred_element_type=jnp.float32)
    act_low = act_sum.astype(jnp.bfloat16)
    for copy in copies[2:]:
        copy.wait()
    grad_sum = lax.dot_general(grad_proj[...], grads[...], NT, preferred_element_type=jnp.float32)
    rank, seq_len = grad_sum.shape
    turned[pl.ds(0, rank), :] = grad_sum * keep_ref[...]
    halves = [
        jnp.dot(
            turned[pl.ds(side, rank // 2, stride=2), :].astype(jnp.bfloat16),
            act_low,
            preferred_element_type=jnp.float32,
        )
        for side in range(2)
    ]
    outer = jnp.concatenate(halves, axis=1) * (1.0 / math.sqrt(seq_len))
    out_ref[...] = outer.astype(jnp.bfloat16)


def make_sketch(acts, grads, act_proj, grad_proj, tok_count):
    seq_len, rank = acts.shape[0], act_proj.shape[1]
    operands = (acts, grads, act_proj.T, grad_proj.T)
    keep = (jnp.arange(seq_len, dtype=jnp.int32) < tok_count).astype(jnp.float32)
    vmem = pl.BlockSpec(memory_space=pltpu.VMEM)
    return pl.pallas_call(
        sketch_kernel,
        out_shape=jax.ShapeDtypeStruct((rank // 2, 2 * rank), jnp.bfloat16),
        in_specs=[pl.BlockSpec(memory_space=pl.ANY)] * 4 + [vmem],
        out_specs=vmem,
        scratch_shapes=[pltpu.VMEM(x.shape, x.dtype) for x in operands]
        + [pltpu.VMEM((rank + 8, seq_len), jnp.float32), pltpu.SemaphoreType.DMA((4,))],
        compiler_params=pltpu.CompilerParams(vmem_limit_bytes=16 * 2**20),
        name="sketch",
    )(*[pltpu.with_memory_space_constraint(x, pltpu.HBM) for x in operands], keep[None])


def spread(block, distances):
    pairs = [
        (e * len(distances) + p, (e ^ k) * len(distances) + p)
        for e in range(lax.axis_size("ex"))
        for p, k in enumerate(distances)
    ]
    return lax.ppermute(block, ("ex", "pb"), pairs)


def take(block, index):
    return lax.dynamic_index_in_dim(block, index, 1, keepdims=False)


def pairs_of_distances(ex_count):
    return [(k, min(k + 1, ex_count - 1)) for k in range(1, ex_count, 2)]


def gather_rows(sizes, sketch, queries):
    ex_count, feat_count, pb_count = sizes
    ex, feat, pb = (lax.axis_index(axis) for axis in ("ex", "feat", "pb"))
    fp_count, fp = feat_count * pb_count, feat * pb_count + pb
    ratio = ex_count // fp_count
    own = sketch.reshape(1, ex_count, -1, LANES)
    own = jnp.concatenate([own, exchange(own, "pb", 1)])
    own, queries = lax.optimization_barrier((own, queries))
    others = exchange(queries, "pb", 1)
    line = [own]
    for k in range(1, feat_count):
        line.append(exchange(own, ("feat", "pb"), k * pb_count + 1)[::-1])
    block = jnp.concatenate(line)
    by_fp = block.reshape(fp_count, fp_count, ratio, -1, LANES)

    def columns(index):
        return jnp.moveaxis(take(by_fp, index), 1, 0)

    pieces = [(block, (0, 0), 0, None)]
    for near, far in pairs_of_distances(ex_count):
        theirs = take(block, ex ^ (near + (far - near) * pb))[None]
        if near == far:
            rows = spread(jnp.concatenate([theirs, columns(fp)]), (near, far))
            pieces.append((rows, (near, far), 0, 0))
        else:
            rows = jnp.concatenate([columns(fp), theirs, columns(fp ^ 1)])
            rows = spread(rows, (near, far))
            pieces.append((rows, (near, far), 0, ratio))
            pieces.append((exchange(rows[ratio:], "pb", 1), (far, near), 1, 0))
    return pieces, others


def place_rows(sizes, origins, pieces, left_rows, right_rows=None):
    ex_count, feat_count, pb_count = sizes
    ex, pb = lax.axis_index("ex"), lax.axis_index("pb")
    fp_count = feat_count * pb_count
    ratio = ex_count // fp_count
    fp = lax.axis_index("feat") * pb_count + pb
    for piece, (distances, other, left) in zip(pieces, origins):
        where = ex ^ (distances[0] + (distances[1] - distances[0]) * pb)
        for s in range(fp_count):
            slot = (fp ^ other ^ s) * ex_count + where
            block = piece[s, ex] if left is None else piece[left, s]
            left_rows[slot] = block.astype(jnp.float32)
            if right_rows is not None:
                if left is None:
                    block = piece[s, pl.ds(fp * ratio, ratio)]
                else:
                    right = 0 if left else 1
                    block = piece[right : right + ratio, s]
                right_rows[slot] = block.astype(jnp.float32).reshape(right_rows.shape[1:])


def score_kernel(sizes, origins, query_ref, other_query_ref, *refs):
    ex_count, feat_count, pb_count = sizes
    pieces, refs = refs[: len(origins)], refs[len(origins) :]
    half = ex_count // pb_count
    outs = refs[:half]
    own_ref, rows, scaled, chunks = refs[-4:]
    ex, feat = lax.axis_index("ex"), lax.axis_index("feat")
    near = lax.axis_index("pb") == 0
    here = lax.rem(ex, half)
    examples, block_lines, lanes = rows.shape
    mine = ex_count * pb_count
    width = chunks.shape[2]
    for side, queries in enumerate((query_ref, other_query_ref)):

        @pl.when(lax.div(ex, half) == side)
        def _():
            place_rows(sizes, origins, pieces, rows)
            diag = jnp.sum(rows[...] * rows[...], axis=0) / examples
            weight = 1.0 / (math.sqrt(ex_count * block_lines * lanes) * (diag + DAMPING))
            own = rows[pl.ds(feat * mine, mine)]
            scaled[pl.ds(0, mine * block_lines), :] = (own * weight[None]).reshape(
                mine * block_lines, lanes
            )
            parts = [scaled[pl.ds(j, mine, stride=block_lines), :] for j in range(block_lines)]
            wide = jnp.concatenate(parts, axis=1)
            high = wide.astype(jnp.bfloat16)
            low = (wide - high.astype(jnp.float32)).astype(jnp.bfloat16)
            both = jnp.concatenate([high, low], axis=0)
            products = lax.dot_general(
                both, queries[...], NT, preferred_element_type=jnp.float32
            )
            result = products[:mine] + products[mine:]
            for t in range(half):
                chunks[t] = result[:, t * width : (t + 1) * width]

    shift = near.astype(jnp.int32)
    for i in range(half - 1):
        outs[i][...] = chunks[here ^ (i + shift)]
    outs[half - 1][...] = jnp.where(near, 0.0, chunks[here ^ (half - 1)])
    own_ref[...] = jnp.where(near, chunks[here], 0.0)


def partial_scores(sizes, queries, other_queries, pieces):
    ex_count, feat_count, pb_count = sizes
    examples = ex_count * feat_count * pb_count
    lines, lanes = pieces[0][0].shape[2:]
    half = ex_count // pb_count
    chunk = (pb_count * ex_count, queries.shape[0] // half)
    vmem = pl.BlockSpec(memory_space=pltpu.VMEM)
    return pl.pallas_call(
        functools.partial(score_kernel, sizes, [piece[1:] for piece in pieces]),
        out_shape=[jax.ShapeDtypeStruct(chunk, jnp.float32)] * (half + 1),
        in_specs=[vmem] * (2 + len(pieces)),
        out_specs=[vmem] * (half + 1),
        scratch_shapes=[
            pltpu.VMEM((examples, lines, lanes), jnp.float32),
            pltpu.VMEM(((pb_count * ex_count + 1) * lines, lanes), jnp.float32),
            pltpu.VMEM((half, *chunk), jnp.float32),
        ],
        compiler_params=pltpu.CompilerParams(vmem_limit_bytes=24 * 2**20),
        name="scores",
    )(queries, other_queries, *[piece[0] for piece in pieces])


def gram_kernel(sizes, origins, kept_ref, query_ids_ref, example_ids_ref, *refs):
    pieces, refs = refs[: len(origins)], refs[len(origins) :]
    out_hbm, kept_out_ref, open_ref, left_rows, right_rows, left, right, result, sems = refs
    kept_out_ref[...] = kept_ref[...]
    ex = lax.axis_index("ex")
    spans = open_ref.shape[2] // query_ids_ref.shape[1]
    ids = [query_ids_ref[pl.ds(ex * spans + i, 1), :] for i in range(spans)]
    ids = jnp.concatenate(ids, axis=1)
    for a in range(open_ref.shape[0]):
        open_ref[a] = jnp.where(example_ids_ref[:, a : a + 1] == ids, 0.0, 1.0)
    examples, left_lines, lanes = left_rows.shape
    right_lines = right_rows.shape[1]
    place_rows(sizes, origins, pieces, left_rows, right_rows)
    for rows, flat in ((left_rows, left), (right_rows, right)):
        lines = examples * rows.shape[1]
        flat[pl.ds(0, lines), :] = rows[...].reshape(lines, lanes)
    across = jnp.concatenate(
        [right[pl.ds(j, examples, stride=right_lines), :] for j in range(right_lines)], axis=1
    ).astype(jnp.bfloat16)
    copies = []
    for i in range(left_lines):
        here = left[pl.ds(i, examples, stride=left_lines), :].T.astype(jnp.bfloat16)
        band = pl.ds(i * lanes, lanes)
        total = jnp.dot(here, across, preferred_element_type=jnp.float32)
        result[band, :] = total * (1.0 / examples)
        copies.append(
            pltpu.make_async_copy(result.at[band, :], out_hbm.at[band, :], sems.at[i])
        )
        copies[-1].start()
    for copy in copies:
        copy.wait()


def make_gram(sizes, pieces, kept, query_ids, example_ids):
    examples = sizes[0] * sizes[1] * sizes[2]
    left_lines = pieces[0][0].shape[2]
    right_lines = left_lines * sizes[0] // (sizes[1] * sizes[2])
    shape = (left_lines * LANES, right_lines * LANES)
    vmem = pl.BlockSpec(memory_space=pltpu.VMEM)
    return pl.pallas_call(
        functools.partial(gram_kernel, sizes, [piece[1:] for piece in pieces]),
        out_shape=[
            jax.ShapeDtypeStruct(shape, jnp.float32),
            jax.ShapeDtypeStruct(kept.shape, kept.dtype),
            jax.ShapeDtypeStruct((sizes[0], 1, kept.shape[1]), jnp.float32),
        ],
        in_specs=[vmem] * (3 + len(pieces)),
        out_specs=[pl.BlockSpec(memory_space=pl.ANY), vmem, vmem],
        scratch_shapes=[
            pltpu.VMEM((examples, left_lines, LANES), jnp.float32),
            pltpu.VMEM((examples, right_lines, LANES), jnp.float32),
            pltpu.VMEM(((examples + 1) * left_lines, LANES), jnp.float32),
            pltpu.VMEM(((examples + 1) * right_lines, LANES), jnp.float32),
            pltpu.VMEM(shape, jnp.float32),
            pltpu.SemaphoreType.DMA((left_lines,)),
        ],
        compiler_params=pltpu.CompilerParams(vmem_limit_bytes=24 * 2**20),
        cost_estimate=pl.CostEstimate(
            flops=2 * 256 * shape[0] * shape[1],
            bytes_accessed=4 * shape[0] * shape[1],
            transcendentals=0,
        ),
        name="gram",
    )(kept, query_ids, example_ids, *[piece[0] for piece in pieces])


def to_owners(chunks, sizes):
    ex_count, feat_count, pb_count = sizes
    half = ex_count // pb_count

    def device(e, f, p):
        return (e * feat_count + f) * pb_count + p

    arrived = []
    for i, chunk in enumerate(chunks):
        pairs = []
        for e in range(ex_count):
            for f in range(feat_count):
                near = device(e ^ (i + 1), f, 0) if i < half - 1 else device(e, f ^ 1, 0)
                pairs.append((device(e, f, 0), near))
                pairs.append((device(e, f, 1), device(e ^ (half + i), f, 1)))
        arrived.append(lax.ppermute(chunk, ("ex", "feat", "pb"), pairs))
    return sum(arrived)


def shards(
    activations, out_grads, act_proj, grad_proj, tok_counts, example_ids, query_sketch, query_ids
):
    ex_count, feat_count, pb_count = (lax.axis_size(axis) for axis in ("ex", "feat", "pb"))
    sizes = (ex_count, feat_count, pb_count)
    sketch = make_sketch(
        activations[0, 0], out_grads[0, 0], act_proj, grad_proj, tok_counts[0, 0]
    )
    pieces, others = gather_rows(sizes, sketch, query_sketch)
    width = query_ids.shape[0] // ex_count
    ids = query_ids.reshape(-1, min(width, 128))
    *chunks, own = partial_scores(sizes, query_sketch, others, pieces)
    part = to_owners(chunks, sizes)
    gram, own, is_open = make_gram(sizes, pieces, own, ids, example_ids.T)
    part = (part + own).reshape(pb_count, ex_count, 1, -1)
    pb = lax.axis_index("pb")
    theirs = lax.dynamic_index_in_dim(part, 1 - pb, 0, keepdims=False)
    total = lax.dynamic_index_in_dim(part, pb, 0, keepdims=False) + exchange(theirs, "pb", 1)
    scores = jnp.where(is_open == 0.0, jnp.float32(0.0), total)
    return gram, scores.transpose(2, 0, 1)


def solution(mesh):
    return jax.shard_map(
        shards,
        mesh=mesh,
        in_specs=(
            P(("groups", "ex"), ("feat", "pb"), None, None),
            P(("groups", "ex"), ("feat", "pb"), None, None),
            P(),
            P(),
            P(("groups", "ex"), ("feat", "pb")),
            P("groups", ("feat", "pb")),
            P(("groups", "pb"), "ex"),
            P("groups"),
        ),
        out_specs=(P(("groups", "ex"), ("feat", "pb")), P(("groups", "ex"), None, ("feat", "pb"))),
        check_vma=False,
    )
```

```python
import functools
import math

import jax
import jax.numpy as jnp
from jax import lax
from jax.experimental import pallas as pl
from jax.experimental.pallas import tpu as pltpu
from jax.sharding import PartitionSpec as P

DAMPING = 0.1
LANES = 128
NT = (((1,), (1,)), ((), ()))


def exchange(block, axis, step):
    return lax.ppermute(block, axis, [(i, i ^ step) for i in range(lax.axis_size(axis))])


def sketch_kernel(
    acts_hbm, grads_hbm, act_proj_hbm, grad_proj_hbm, keep_ref, out_ref,
    acts, grads, act_proj, grad_proj, turned, sems,
):
    sources = (act_proj_hbm, acts_hbm, grad_proj_hbm, grads_hbm)
    targets = (act_proj, acts, grad_proj, grads)
    copies = [
        pltpu.make_async_copy(s, t, sems.at[i]) for i, (s, t) in enumerate(zip(sources, targets))
    ]
    for copy, priority in zip(copies, (0, 0, 1, 0)):
        copy.start(priority=priority)
    for copy in copies[:2]:
        copy.wait()
    act_sum = lax.dot_general(acts[...], act_proj[...], NT, preferred_element_type=jnp.float32)
    act_low = act_sum.astype(jnp.bfloat16)
    for copy in copies[2:]:
        copy.wait()
    grad_sum = lax.dot_general(grad_proj[...], grads[...], NT, preferred_element_type=jnp.float32)
    rank, seq_len = grad_sum.shape
    turned[pl.ds(0, rank), :] = grad_sum * keep_ref[...]
    halves = [
        jnp.dot(
            turned[pl.ds(side, rank // 2, stride=2), :].astype(jnp.bfloat16),
            act_low,
            preferred_element_type=jnp.float32,
        )
        for side in range(2)
    ]
    outer = jnp.concatenate(halves, axis=1) * (1.0 / math.sqrt(seq_len))
    out_ref[...] = outer.astype(jnp.bfloat16)


def make_sketch(acts, grads, act_proj, grad_proj, tok_count):
    seq_len, rank = acts.shape[0], act_proj.shape[1]
    operands = (acts, grads, act_proj.T, grad_proj.T)
    keep = (jnp.arange(seq_len, dtype=jnp.int32) < tok_count).astype(jnp.float32)
    vmem = pl.BlockSpec(memory_space=pltpu.VMEM)
    return pl.pallas_call(
        sketch_kernel,
        out_shape=jax.ShapeDtypeStruct((rank // 2, 2 * rank), jnp.bfloat16),
        in_specs=[pl.BlockSpec(memory_space=pl.ANY)] * 4 + [vmem],
        out_specs=vmem,
        scratch_shapes=[pltpu.VMEM(x.shape, x.dtype) for x in operands]
        + [pltpu.VMEM((rank + 8, seq_len), jnp.float32), pltpu.SemaphoreType.DMA((4,))],
        compiler_params=pltpu.CompilerParams(vmem_limit_bytes=16 * 2**20),
        name="sketch",
    )(*[pltpu.with_memory_space_constraint(x, pltpu.HBM) for x in operands], keep[None])


def spread(block, distances):
    pairs = [
        (e * len(distances) + p, (e ^ k) * len(distances) + p)
        for e in range(lax.axis_size("ex"))
        for p, k in enumerate(distances)
    ]
    return lax.ppermute(block, ("ex", "pb"), pairs)


def take(block, index):
    return lax.dynamic_index_in_dim(block, index, 1, keepdims=False)


def pairs_of_distances(ex_count):
    return [(k, min(k + 1, ex_count - 1)) for k in range(1, ex_count, 2)]


def gather_rows(sizes, sketch, queries):
    ex_count, feat_count, pb_count = sizes
    ex, feat, pb = (lax.axis_index(axis) for axis in ("ex", "feat", "pb"))
    fp_count, fp = feat_count * pb_count, feat * pb_count + pb
    ratio = ex_count // fp_count
    own = sketch.reshape(1, ex_count, -1, LANES)
    own = jnp.concatenate([own, exchange(own, "pb", 1)])
    own, queries = lax.optimization_barrier((own, queries))
    others = exchange(queries, "pb", 1)
    line = [own]
    for k in range(1, feat_count):
        line.append(exchange(own, ("feat", "pb"), k * pb_count + 1)[::-1])
    block = jnp.concatenate(line)
    by_fp = block.reshape(fp_count, fp_count, ratio, -1, LANES)

    def columns(index):
        return jnp.moveaxis(take(by_fp, index), 1, 0)

    pieces = [(block, (0, 0), 0, None)]
    for near, far in pairs_of_distances(ex_count):
        theirs = take(block, ex ^ (near + (far - near) * pb))[None]
        if near == far:
            rows = spread(jnp.concatenate([theirs, columns(fp)]), (near, far))
            pieces.append((rows, (near, far), 0, 0))
        else:
            rows = jnp.concatenate([columns(fp), theirs, columns(fp ^ 1)])
            rows = spread(rows, (near, far))
            pieces.append((rows, (near, far), 0, ratio))
            pieces.append((exchange(rows[ratio:], "pb", 1), (far, near), 1, 0))
    return pieces, others


def place_rows(sizes, origins, pieces, left_rows, right_rows=None):
    ex_count, feat_count, pb_count = sizes
    ex, pb = lax.axis_index("ex"), lax.axis_index("pb")
    fp_count = feat_count * pb_count
    ratio = ex_count // fp_count
    fp = lax.axis_index("feat") * pb_count + pb
    for piece, (distances, other, left) in zip(pieces, origins):
        where = ex ^ (distances[0] + (distances[1] - distances[0]) * pb)
        for s in range(fp_count):
            slot = (fp ^ other ^ s) * ex_count + where
            block = piece[s, ex] if left is None else piece[left, s]
            left_rows[slot] = block.astype(jnp.float32)
            if right_rows is not None:
                if left is None:
                    block = piece[s, pl.ds(fp * ratio, ratio)]
                else:
                    right = 0 if left else 1
                    block = piece[right : right + ratio, s]
                right_rows[slot] = block.astype(jnp.float32).reshape(right_rows.shape[1:])


def score_kernel(sizes, origins, query_ref, other_query_ref, *refs):
    ex_count, feat_count, pb_count = sizes
    pieces, refs = refs[: len(origins)], refs[len(origins) :]
    half = ex_count // pb_count
    outs = refs[:half]
    own_ref, rows, scaled, chunks = refs[-4:]
    ex, feat = lax.axis_index("ex"), lax.axis_index("feat")
    near = lax.axis_index("pb") == 0
    here = lax.rem(ex, half)
    examples, block_lines, lanes = rows.shape
    mine = ex_count * pb_count
    width = chunks.shape[2]
    for side, queries in enumerate((query_ref, other_query_ref)):

        @pl.when(lax.div(ex, half) == side)
        def _():
            place_rows(sizes, origins, pieces, rows)
            diag = jnp.sum(rows[...] * rows[...], axis=0) / examples
            weight = 1.0 / (math.sqrt(ex_count * block_lines * lanes) * (diag + DAMPING))
            own = rows[pl.ds(feat * mine, mine)]
            scaled[pl.ds(0, mine * block_lines), :] = (own * weight[None]).reshape(
                mine * block_lines, lanes
            )
            parts = [scaled[pl.ds(j, mine, stride=block_lines), :] for j in range(block_lines)]
            wide = jnp.concatenate(parts, axis=1)
            high = wide.astype(jnp.bfloat16)
            low = (wide - high.astype(jnp.float32)).astype(jnp.bfloat16)
            both = jnp.concatenate([high, low], axis=0)
            for t in range(half):
                products = lax.dot_general(
                    both,
                    queries[t * width : (t + 1) * width, :],
                    NT,
                    preferred_element_type=jnp.float32,
                )
                chunks[t] = products[:mine] + products[mine:]

    shift = near.astype(jnp.int32)
    for i in range(half - 1):
        outs[i][...] = chunks[here ^ (i + shift)]
    outs[half - 1][...] = jnp.where(near, 0.0, chunks[here ^ (half - 1)])
    own_ref[...] = jnp.where(near, chunks[here], 0.0)


def partial_scores(sizes, queries, other_queries, pieces):
    ex_count, feat_count, pb_count = sizes
    examples = ex_count * feat_count * pb_count
    lines, lanes = pieces[0][0].shape[2:]
    half = ex_count // pb_count
    chunk = (pb_count * ex_count, queries.shape[0] // half)
    vmem = pl.BlockSpec(memory_space=pltpu.VMEM)
    return pl.pallas_call(
        functools.partial(score_kernel, sizes, [piece[1:] for piece in pieces]),
        out_shape=[jax.ShapeDtypeStruct(chunk, jnp.float32)] * (half + 1),
        in_specs=[vmem] * (2 + len(pieces)),
        out_specs=[vmem] * (half + 1),
        scratch_shapes=[
            pltpu.VMEM((examples, lines, lanes), jnp.float32),
            pltpu.VMEM(((pb_count * ex_count + 1) * lines, lanes), jnp.float32),
            pltpu.VMEM((half, *chunk), jnp.float32),
        ],
        compiler_params=pltpu.CompilerParams(vmem_limit_bytes=24 * 2**20),
        name="scores",
    )(queries, other_queries, *[piece[0] for piece in pieces])


def gram_kernel(sizes, origins, kept_ref, query_ids_ref, example_ids_ref, *refs):
    pieces, refs = refs[: len(origins)], refs[len(origins) :]
    out_hbm, kept_out_ref, open_ref, left_rows, right_rows, left, right, result, sems = refs
    kept_out_ref[...] = kept_ref[...]
    ex = lax.axis_index("ex")
    spans = open_ref.shape[2] // query_ids_ref.shape[1]
    ids = [query_ids_ref[pl.ds(ex * spans + i, 1), :] for i in range(spans)]
    ids = jnp.concatenate(ids, axis=1)
    for a in range(open_ref.shape[0]):
        open_ref[a] = jnp.where(example_ids_ref[:, a : a + 1] == ids, 0.0, 1.0)
    examples, left_lines, lanes = left_rows.shape
    right_lines = right_rows.shape[1]
    place_rows(sizes, origins, pieces, left_rows, right_rows)
    for rows, flat in ((left_rows, left), (right_rows, right)):
        lines = examples * rows.shape[1]
        flat[pl.ds(0, lines), :] = rows[...].reshape(lines, lanes)
    across = jnp.concatenate(
        [right[pl.ds(j, examples, stride=right_lines), :] for j in range(right_lines)], axis=1
    ).astype(jnp.bfloat16)
    copies = []
    for i in range(left_lines):
        here = left[pl.ds(i, examples, stride=left_lines), :].T.astype(jnp.bfloat16)
        band = pl.ds(i * lanes, lanes)
        total = jnp.dot(here, across, preferred_element_type=jnp.float32)
        result[band, :] = total * (1.0 / examples)
        copies.append(
            pltpu.make_async_copy(result.at[band, :], out_hbm.at[band, :], sems.at[i])
        )
        copies[-1].start()
    for copy in copies:
        copy.wait()


def make_gram(sizes, pieces, kept, query_ids, example_ids):
    examples = sizes[0] * sizes[1] * sizes[2]
    left_lines = pieces[0][0].shape[2]
    right_lines = left_lines * sizes[0] // (sizes[1] * sizes[2])
    shape = (left_lines * LANES, right_lines * LANES)
    vmem = pl.BlockSpec(memory_space=pltpu.VMEM)
    return pl.pallas_call(
        functools.partial(gram_kernel, sizes, [piece[1:] for piece in pieces]),
        out_shape=[
            jax.ShapeDtypeStruct(shape, jnp.float32),
            jax.ShapeDtypeStruct(kept.shape, kept.dtype),
            jax.ShapeDtypeStruct((sizes[0], 1, kept.shape[1]), jnp.float32),
        ],
        in_specs=[vmem] * (3 + len(pieces)),
        out_specs=[pl.BlockSpec(memory_space=pl.ANY), vmem, vmem],
        scratch_shapes=[
            pltpu.VMEM((examples, left_lines, LANES), jnp.float32),
            pltpu.VMEM((examples, right_lines, LANES), jnp.float32),
            pltpu.VMEM(((examples + 1) * left_lines, LANES), jnp.float32),
            pltpu.VMEM(((examples + 1) * right_lines, LANES), jnp.float32),
            pltpu.VMEM(shape, jnp.float32),
            pltpu.SemaphoreType.DMA((left_lines,)),
        ],
        compiler_params=pltpu.CompilerParams(vmem_limit_bytes=24 * 2**20),
        cost_estimate=pl.CostEstimate(
            flops=2 * 256 * shape[0] * shape[1],
            bytes_accessed=4 * shape[0] * shape[1],
            transcendentals=0,
        ),
        name="gram",
    )(kept, query_ids, example_ids, *[piece[0] for piece in pieces])


def to_owners(chunks, sizes):
    ex_count, feat_count, pb_count = sizes
    half = ex_count // pb_count

    def device(e, f, p):
        return (e * feat_count + f) * pb_count + p

    arrived = []
    for i, chunk in enumerate(chunks):
        pairs = []
        for e in range(ex_count):
            for f in range(feat_count):
                near = device(e ^ (i + 1), f, 0) if i < half - 1 else device(e, f ^ 1, 0)
                pairs.append((device(e, f, 0), near))
                pairs.append((device(e, f, 1), device(e ^ (half + i), f, 1)))
        arrived.append(lax.ppermute(chunk, ("ex", "feat", "pb"), pairs))
    return sum(arrived)


def shards(
    activations, out_grads, act_proj, grad_proj, tok_counts, example_ids, query_sketch, query_ids
):
    ex_count, feat_count, pb_count = (lax.axis_size(axis) for axis in ("ex", "feat", "pb"))
    sizes = (ex_count, feat_count, pb_count)
    sketch = make_sketch(
        activations[0, 0], out_grads[0, 0], act_proj, grad_proj, tok_counts[0, 0]
    )
    pieces, others = gather_rows(sizes, sketch, query_sketch)
    width = query_ids.shape[0] // ex_count
    ids = query_ids.reshape(-1, min(width, 128))
    *chunks, own = partial_scores(sizes, query_sketch, others, pieces)
    part = to_owners(chunks, sizes)
    gram, own, is_open = make_gram(sizes, pieces, own, ids, example_ids.T)
    part = (part + own).reshape(pb_count, ex_count, 1, -1)
    pb = lax.axis_index("pb")
    theirs = lax.dynamic_index_in_dim(part, 1 - pb, 0, keepdims=False)
    total = lax.dynamic_index_in_dim(part, pb, 0, keepdims=False) + exchange(theirs, "pb", 1)
    scores = jnp.where(is_open == 0.0, jnp.float32(0.0), total)
    return gram, scores.transpose(2, 0, 1)


def solution(mesh):
    return jax.shard_map(
        shards,
        mesh=mesh,
        in_specs=(
            P(("groups", "ex"), ("feat", "pb"), None, None),
            P(("groups", "ex"), ("feat", "pb"), None, None),
            P(),
            P(),
            P(("groups", "ex"), ("feat", "pb")),
            P("groups", ("feat", "pb")),
            P(("groups", "pb"), "ex"),
            P("groups"),
        ),
        out_specs=(P(("groups", "ex"), ("feat", "pb")), P(("groups", "ex"), None, ("feat", "pb"))),
        check_vma=False,
    )
```

```python
import functools
import math

import jax
import jax.numpy as jnp
from jax import lax
from jax.experimental import pallas as pl
from jax.experimental.pallas import tpu as pltpu
from jax.sharding import PartitionSpec as P

DAMPING = 0.1
LANES = 128
NT = (((1,), (1,)), ((), ()))


def exchange(block, axis, step):
    return lax.ppermute(block, axis, [(i, i ^ step) for i in range(lax.axis_size(axis))])


def sketch_kernel(
    acts_hbm, grads_hbm, act_proj_hbm, grad_proj_hbm, keep_ref, out_ref,
    acts, grads, act_proj, grad_proj, turned, sems,
):
    rows = grads.shape[0] // 2
    parts = [pl.ds(c * rows, rows) for c in range(2)]
    sources = (act_proj_hbm, acts_hbm, grad_proj_hbm, *(grads_hbm.at[part, :] for part in parts))
    targets = (act_proj, acts, grad_proj, *(grads.at[part, :] for part in parts))
    copies = [
        pltpu.make_async_copy(s, t, sems.at[i]) for i, (s, t) in enumerate(zip(sources, targets))
    ]
    for copy, priority in zip(copies, (0, 0, 0, 0, 0)):
        copy.start(priority=priority)
    for copy in copies[:2]:
        copy.wait()
    act_sum = lax.dot_general(acts[...], act_proj[...], NT, preferred_element_type=jnp.float32)
    act_low = act_sum.astype(jnp.bfloat16)
    copies[2].wait()
    rank, seq_len = act_proj.shape[0], grads.shape[0]
    for part, copy in zip(parts, copies[3:]):
        copy.wait()
        grad_sum = lax.dot_general(
            grad_proj[...], grads[part, :], NT, preferred_element_type=jnp.float32
        )
        turned[pl.ds(0, rank), part] = grad_sum * keep_ref[:, part]
    halves = [
        jnp.dot(
            turned[pl.ds(side, rank // 2, stride=2), :].astype(jnp.bfloat16),
            act_low,
            preferred_element_type=jnp.float32,
        )
        for side in range(2)
    ]
    outer = jnp.concatenate(halves, axis=1) * (1.0 / math.sqrt(seq_len))
    out_ref[...] = outer.astype(jnp.bfloat16)


def make_sketch(acts, grads, act_proj, grad_proj, tok_count):
    seq_len, rank = acts.shape[0], act_proj.shape[1]
    operands = (acts, grads, act_proj.T, grad_proj.T)
    keep = (jnp.arange(seq_len, dtype=jnp.int32) < tok_count).astype(jnp.float32)
    vmem = pl.BlockSpec(memory_space=pltpu.VMEM)
    return pl.pallas_call(
        sketch_kernel,
        out_shape=jax.ShapeDtypeStruct((rank // 2, 2 * rank), jnp.bfloat16),
        in_specs=[pl.BlockSpec(memory_space=pl.ANY)] * 4 + [vmem],
        out_specs=vmem,
        scratch_shapes=[pltpu.VMEM(x.shape, x.dtype) for x in operands]
        + [pltpu.VMEM((rank + 8, seq_len), jnp.float32), pltpu.SemaphoreType.DMA((5,))],
        compiler_params=pltpu.CompilerParams(vmem_limit_bytes=16 * 2**20),
        name="sketch",
    )(*[pltpu.with_memory_space_constraint(x, pltpu.HBM) for x in operands], keep[None])


def spread(block, distances):
    pairs = [
        (e * len(distances) + p, (e ^ k) * len(distances) + p)
        for e in range(lax.axis_size("ex"))
        for p, k in enumerate(distances)
    ]
    return lax.ppermute(block, ("ex", "pb"), pairs)


def take(block, index):
    return lax.dynamic_index_in_dim(block, index, 1, keepdims=False)


def pairs_of_distances(ex_count):
    return [(k, min(k + 1, ex_count - 1)) for k in range(1, ex_count, 2)]


def gather_rows(sizes, sketch, queries):
    ex_count, feat_count, pb_count = sizes
    ex, feat, pb = (lax.axis_index(axis) for axis in ("ex", "feat", "pb"))
    fp_count, fp = feat_count * pb_count, feat * pb_count + pb
    ratio = ex_count // fp_count
    own = sketch.reshape(1, ex_count, -1, LANES)
    own = jnp.concatenate([own, exchange(own, "pb", 1)])
    own, queries = lax.optimization_barrier((own, queries))
    others = exchange(queries, "pb", 1)
    line = [own]
    for k in range(1, feat_count):
        line.append(exchange(own, ("feat", "pb"), k * pb_count + 1)[::-1])
    block = jnp.concatenate(line)
    by_fp = block.reshape(fp_count, fp_count, ratio, -1, LANES)

    def columns(index):
        return jnp.moveaxis(take(by_fp, index), 1, 0)

    pieces = [(block, (0, 0), 0, None)]
    for near, far in pairs_of_distances(ex_count):
        theirs = take(block, ex ^ (near + (far - near) * pb))[None]
        if near == far:
            rows = spread(jnp.concatenate([theirs, columns(fp)]), (near, far))
            pieces.append((rows, (near, far), 0, 0))
        else:
            rows = jnp.concatenate([columns(fp), theirs, columns(fp ^ 1)])
            rows = spread(rows, (near, far))
            pieces.append((rows, (near, far), 0, ratio))
            pieces.append((exchange(rows[ratio:], "pb", 1), (far, near), 1, 0))
    return pieces, others


def place_rows(sizes, origins, pieces, left_rows, right_rows=None):
    ex_count, feat_count, pb_count = sizes
    ex, pb = lax.axis_index("ex"), lax.axis_index("pb")
    fp_count = feat_count * pb_count
    ratio = ex_count // fp_count
    fp = lax.axis_index("feat") * pb_count + pb
    for piece, (distances, other, left) in zip(pieces, origins):
        where = ex ^ (distances[0] + (distances[1] - distances[0]) * pb)
        for s in range(fp_count):
            slot = (fp ^ other ^ s) * ex_count + where
            block = piece[s, ex] if left is None else piece[left, s]
            left_rows[slot] = block.astype(jnp.float32)
            if right_rows is not None:
                if left is None:
                    block = piece[s, pl.ds(fp * ratio, ratio)]
                else:
                    right = 0 if left else 1
                    block = piece[right : right + ratio, s]
                right_rows[slot] = block.astype(jnp.float32).reshape(right_rows.shape[1:])


def score_kernel(sizes, origins, query_ref, other_query_ref, *refs):
    ex_count, feat_count, pb_count = sizes
    pieces, refs = refs[: len(origins)], refs[len(origins) :]
    half = ex_count // pb_count
    outs = refs[:half]
    own_ref, rows, scaled, chunks = refs[-4:]
    ex, feat = lax.axis_index("ex"), lax.axis_index("feat")
    near = lax.axis_index("pb") == 0
    here = lax.rem(ex, half)
    examples, block_lines, lanes = rows.shape
    mine = ex_count * pb_count
    width = chunks.shape[2]
    for side, queries in enumerate((query_ref, other_query_ref)):

        @pl.when(lax.div(ex, half) == side)
        def _():
            place_rows(sizes, origins, pieces, rows)
            diag = jnp.sum(rows[...] * rows[...], axis=0) / examples
            weight = 1.0 / (math.sqrt(ex_count * block_lines * lanes) * (diag + DAMPING))
            own = rows[pl.ds(feat * mine, mine)]
            scaled[pl.ds(0, mine * block_lines), :] = (own * weight[None]).reshape(
                mine * block_lines, lanes
            )
            parts = [scaled[pl.ds(j, mine, stride=block_lines), :] for j in range(block_lines)]
            wide = jnp.concatenate(parts, axis=1)
            high = wide.astype(jnp.bfloat16)
            low = (wide - high.astype(jnp.float32)).astype(jnp.bfloat16)
            both = jnp.concatenate([high, low], axis=0)
            products = lax.dot_general(
                both, queries[...], NT, preferred_element_type=jnp.float32
            )
            result = products[:mine] + products[mine:]
            for t in range(half):
                chunks[t] = result[:, t * width : (t + 1) * width]

    shift = near.astype(jnp.int32)
    for i in range(half - 1):
        outs[i][...] = chunks[here ^ (i + shift)]
    outs[half - 1][...] = jnp.where(near, 0.0, chunks[here ^ (half - 1)])
    own_ref[...] = jnp.where(near, chunks[here], 0.0)


def partial_scores(sizes, queries, other_queries, pieces):
    ex_count, feat_count, pb_count = sizes
    examples = ex_count * feat_count * pb_count
    lines, lanes = pieces[0][0].shape[2:]
    half = ex_count // pb_count
    chunk = (pb_count * ex_count, queries.shape[0] // half)
    vmem = pl.BlockSpec(memory_space=pltpu.VMEM)
    return pl.pallas_call(
        functools.partial(score_kernel, sizes, [piece[1:] for piece in pieces]),
        out_shape=[jax.ShapeDtypeStruct(chunk, jnp.float32)] * (half + 1),
        in_specs=[vmem] * (2 + len(pieces)),
        out_specs=[vmem] * (half + 1),
        scratch_shapes=[
            pltpu.VMEM((examples, lines, lanes), jnp.float32),
            pltpu.VMEM(((pb_count * ex_count + 1) * lines, lanes), jnp.float32),
            pltpu.VMEM((half, *chunk), jnp.float32),
        ],
        compiler_params=pltpu.CompilerParams(vmem_limit_bytes=24 * 2**20),
        name="scores",
    )(queries, other_queries, *[piece[0] for piece in pieces])


def gram_kernel(sizes, origins, kept_ref, query_ids_ref, example_ids_ref, *refs):
    pieces, refs = refs[: len(origins)], refs[len(origins) :]
    out_hbm, kept_out_ref, open_ref, left_rows, right_rows, left, right, result, sems = refs
    kept_out_ref[...] = kept_ref[...]
    ex = lax.axis_index("ex")
    spans = open_ref.shape[2] // query_ids_ref.shape[1]
    ids = [query_ids_ref[pl.ds(ex * spans + i, 1), :] for i in range(spans)]
    ids = jnp.concatenate(ids, axis=1)
    for a in range(open_ref.shape[0]):
        open_ref[a] = jnp.where(example_ids_ref[:, a : a + 1] == ids, 0.0, 1.0)
    examples, left_lines, lanes = left_rows.shape
    right_lines = right_rows.shape[1]
    place_rows(sizes, origins, pieces, left_rows, right_rows)
    for rows, flat in ((left_rows, left), (right_rows, right)):
        lines = examples * rows.shape[1]
        flat[pl.ds(0, lines), :] = rows[...].reshape(lines, lanes)
    across = jnp.concatenate(
        [right[pl.ds(j, examples, stride=right_lines), :] for j in range(right_lines)], axis=1
    ).astype(jnp.bfloat16)
    copies = []
    for i in range(left_lines):
        here = left[pl.ds(i, examples, stride=left_lines), :].T.astype(jnp.bfloat16)
        band = pl.ds(i * lanes, lanes)
        total = jnp.dot(here, across, preferred_element_type=jnp.float32)
        result[band, :] = total * (1.0 / examples)
        copies.append(
            pltpu.make_async_copy(result.at[band, :], out_hbm.at[band, :], sems.at[i])
        )
        copies[-1].start()
    for copy in copies:
        copy.wait()


def make_gram(sizes, pieces, kept, query_ids, example_ids):
    examples = sizes[0] * sizes[1] * sizes[2]
    left_lines = pieces[0][0].shape[2]
    right_lines = left_lines * sizes[0] // (sizes[1] * sizes[2])
    shape = (left_lines * LANES, right_lines * LANES)
    vmem = pl.BlockSpec(memory_space=pltpu.VMEM)
    return pl.pallas_call(
        functools.partial(gram_kernel, sizes, [piece[1:] for piece in pieces]),
        out_shape=[
            jax.ShapeDtypeStruct(shape, jnp.float32),
            jax.ShapeDtypeStruct(kept.shape, kept.dtype),
            jax.ShapeDtypeStruct((sizes[0], 1, kept.shape[1]), jnp.float32),
        ],
        in_specs=[vmem] * (3 + len(pieces)),
        out_specs=[pl.BlockSpec(memory_space=pl.ANY), vmem, vmem],
        scratch_shapes=[
            pltpu.VMEM((examples, left_lines, LANES), jnp.float32),
            pltpu.VMEM((examples, right_lines, LANES), jnp.float32),
            pltpu.VMEM(((examples + 1) * left_lines, LANES), jnp.float32),
            pltpu.VMEM(((examples + 1) * right_lines, LANES), jnp.float32),
            pltpu.VMEM(shape, jnp.float32),
            pltpu.SemaphoreType.DMA((left_lines,)),
        ],
        compiler_params=pltpu.CompilerParams(vmem_limit_bytes=24 * 2**20),
        cost_estimate=pl.CostEstimate(
            flops=2 * 256 * shape[0] * shape[1],
            bytes_accessed=4 * shape[0] * shape[1],
            transcendentals=0,
        ),
        name="gram",
    )(kept, query_ids, example_ids, *[piece[0] for piece in pieces])


def to_owners(chunks, sizes):
    ex_count, feat_count, pb_count = sizes
    half = ex_count // pb_count

    def device(e, f, p):
        return (e * feat_count + f) * pb_count + p

    arrived = []
    for i, chunk in enumerate(chunks):
        pairs = []
        for e in range(ex_count):
            for f in range(feat_count):
                near = device(e ^ (i + 1), f, 0) if i < half - 1 else device(e, f ^ 1, 0)
                pairs.append((device(e, f, 0), near))
                pairs.append((device(e, f, 1), device(e ^ (half + i), f, 1)))
        arrived.append(lax.ppermute(chunk, ("ex", "feat", "pb"), pairs))
    return sum(arrived)


def shards(
    activations, out_grads, act_proj, grad_proj, tok_counts, example_ids, query_sketch, query_ids
):
    ex_count, feat_count, pb_count = (lax.axis_size(axis) for axis in ("ex", "feat", "pb"))
    sizes = (ex_count, feat_count, pb_count)
    sketch = make_sketch(
        activations[0, 0], out_grads[0, 0], act_proj, grad_proj, tok_counts[0, 0]
    )
    pieces, others = gather_rows(sizes, sketch, query_sketch)
    width = query_ids.shape[0] // ex_count
    ids = query_ids.reshape(-1, min(width, 128))
    *chunks, own = partial_scores(sizes, query_sketch, others, pieces)
    part = to_owners(chunks, sizes)
    gram, own, is_open = make_gram(sizes, pieces, own, ids, example_ids.T)
    part = (part + own).reshape(pb_count, ex_count, 1, -1)
    pb = lax.axis_index("pb")
    theirs = lax.dynamic_index_in_dim(part, 1 - pb, 0, keepdims=False)
    total = lax.dynamic_index_in_dim(part, pb, 0, keepdims=False) + exchange(theirs, "pb", 1)
    scores = jnp.where(is_open == 0.0, jnp.float32(0.0), total)
    return gram, scores.transpose(2, 0, 1)


def solution(mesh):
    return jax.shard_map(
        shards,
        mesh=mesh,
        in_specs=(
            P(("groups", "ex"), ("feat", "pb"), None, None),
            P(("groups", "ex"), ("feat", "pb"), None, None),
            P(),
            P(),
            P(("groups", "ex"), ("feat", "pb")),
            P("groups", ("feat", "pb")),
            P(("groups", "pb"), "ex"),
            P("groups"),
        ),
        out_specs=(P(("groups", "ex"), ("feat", "pb")), P(("groups", "ex"), None, ("feat", "pb"))),
        check_vma=False,
    )
```
